256 devices in a mesh: group: 2 (over core), tensor: 8 (over x, y_lo), seq: 16 (over y_hi, z).
Axes of the slice: x: 4, y: 4 (y_hi: 2, y_lo: 2; y = y_hi * 2 + y_lo), z: 8, core: 2. Of those that a mesh axis runs over, the one named last changes fastest.
Arguments:
- teacher_query: bfloat16 [2, 4096, 8192], P('group', 'seq', 'tensor'), may hold values from -150 to 150
- teacher_keyval: bfloat16 [2, 4096, 2048], P('group', 'seq', 'tensor'), may hold values from -5 to 5
- segment_ids: int32 [4096], P('seq'), may hold values from 0 to 7, never falling along the last dimension, each value on 1 to 2304 neighbouring positions
- projector: bfloat16 [8192, 4096], P('tensor'), may hold values from -0.5 to 0.5
- owner_table: int32 [4096, 1], replicated, may hold values from 0 to 15; in each aligned block of 256 rows (0 to 255, 256 to 511, ...) at most 24 rows name the same one
- student_context: bfloat16 [6144, 4096], P('seq'), may hold values from -6 to 6
- student_out_weight: bfloat16 [4096, 4096], P('seq', 'tensor'), may hold values from -0.09375 to 0.09375
Outputs:
- student_grad: float32 [2, 4096, 4096], P('group', 'seq', 'tensor')
The draws below stay inside these ranges and needn't reach their ends.
Inputs may be any that keep to these rules, and one draw needn't show every extreme that they name: `owner_table`: in each aligned block of 256 rows (the tokens of one teacher shard) no owner appears more than 24 times, and some owner appears exactly 24 times in some block; every owner appears somewhere.
All inputs are finite; a program needn't handle non-finite values.
Results may differ from the reference program's by a relative error of at most 0.025.
Values may be sent and summed in bfloat16 or wider, within the bound.
No kernel may reach another device: no remote copies, remote signals or barrier semaphores. Data moves between devices by JAX's collectives and lax.ppermute only.
A program may use at most 128 MiB of HBM per device.

```python
import math
import jax
import jax.numpy as jnp
import numpy as np
from jax import lax

HT = 64
KVT = 8
HD = 128
DS = 4096
DT = 8192
TOK_DEV = 256
DOCS = 8
TOKENS = 4096
LONGEST = 2304
SLOTS = 384
CAP = 24
N_SEQ = 16


def keys_base(key):
    return jnp.clip(jax.random.normal(key, (2, TOKENS, KVT, HD), jnp.float32), -5.0, 5.0)


def draw_teacher_query(key, part):
    key = jax.random.fold_in(key, 5)
    query_matrix = jnp.clip(jax.random.normal(key, (2, TOKENS, HT, HD), jnp.float32), -5.0, 5.0)
    return query_matrix.reshape(2, TOKENS, HT * HD).astype(jnp.bfloat16)


def draw_teacher_keyval(key, part):
    base = keys_base(key)
    key = jax.random.fold_in(key, 9)
    value_key, offset_key = jax.random.split(key)
    value_matrix = jax.random.normal(value_key, (2, TOKENS, KVT, HD), jnp.float32)
    offsets = 1.5 * jax.random.normal(offset_key, (2, TOKENS // TOK_DEV, KVT, HD), jnp.float32)
    value_matrix = jnp.clip(value_matrix + jnp.repeat(offsets, TOK_DEV, axis=1), -5.0, 5.0)
    key_rows = base
    stacked = jnp.stack([key_rows, value_matrix], axis=3)
    return stacked.reshape(2, TOKENS, KVT * 2 * HD).astype(jnp.bfloat16)


def raised(entries, rng, source, target, shards_of, factor):
    owner, partner = [(jnp.arange(entries.shape[axis_at]) // (entries.shape[axis_at] // shards_of)).reshape([-1 if axis == axis_at else 1 for axis in range(entries.ndim)]) for axis_at in (source, target)]
    chosen = jax.random.permutation(rng, shards_of)[partner]
    strong = (owner == chosen) | (owner == (partner + shards_of // 2) % shards_of)
    return jnp.where(strong, factor * entries, entries)


def levels(own_key, shape, cuts, smallest, top_value):
    def one(position, shards_of):
        draws = jax.random.uniform(jax.random.fold_in(jax.random.fold_in(own_key, 6), position), (shards_of,), jnp.float32, smallest / len(cuts), top_value / len(cuts))
        return jnp.repeat(jnp.exp(draws), shape[position] // shards_of).reshape((-1,) + (1,) * (len(shape) - position - 1))

    loudness = one(*cuts[0])
    for cut in cuts[1:]:
        loudness = loudness * one(*cut)
    return loudness


def split_up(count, total, limit, slope):
    loads = [(1 << 20) // math.isqrt(rank ** slope) + 1 for rank in range(2, count + 1)]
    surplus, given = total - limit - (count - 1), [1] * (count - 1)
    while surplus > 0:
        free = [i for i in range(count - 1) if given[i] < limit]
        mass, left = sum([loads[i] for i in free]), surplus
        for i in free:
            more = min(limit - given[i], max(1, left * loads[i] // mass), surplus)
            given[i] = given[i] + more
            surplus = surplus - more
    return np.array([limit] + given)


def uneven_parts(key, number_of, total, reach, skew):
    if number_of == 2:
        one = jax.random.randint(key, (), max(1, total - reach), min(reach, total - 1) + 1)
        return jnp.stack([one, total - one])
    sizes = jnp.asarray(split_up(number_of, total, reach, skew), jnp.int32)
    pairs = (number_of - 1) // 2
    donor, taker = sizes[1:1 + 2 * pairs:2], sizes[2:2 + 2 * pairs:2]
    room = jnp.minimum(donor - 1, reach - taker)
    passed = jax.random.randint(jax.random.fold_in(key, 1), (pairs,), 0, 1 << 20) % (room + 1)
    sizes = sizes.at[1:1 + 2 * pairs:2].set(donor - passed).at[2:2 + 2 * pairs:2].set(taker + passed)
    return sizes[jax.random.permutation(jax.random.fold_in(key, 2), number_of)]


def shared_out(own_key, own, number, rows, count, top, bound, skew):
    sequence = jax.random.permutation(own_key, count)
    packed, usual = shares(count, rows * top, bound, skew, True), shares(count, rows * top, bound, skew, False)
    places = jnp.arange(count)

    def named(lengths, rotation):
        used = int((lengths > 0).sum())
        fixed = max(1, used // 4)
        moved = fixed + (places - fixed + rotation * (used - fixed)) % max(1, count - fixed)
        return jnp.zeros((count,), jnp.int32).at[sequence[jnp.where(places < fixed, places, moved)]].set(jnp.asarray(lengths, jnp.int32))

    lengths = jnp.where(number % 4 == 0, named(packed, number // 4), named(usual, number - number // 4 - 1))
    mixed = jax.random.permutation(jax.random.fold_in(own, 3), count)
    source_of, receiver = mixed[0:count // 2 * 2:2], mixed[1:count // 2 * 2:2]
    slack = jnp.minimum(lengths[source_of] - 1, bound - lengths[receiver]) // 2
    slack = jnp.where((source_of == sequence[0]) | (receiver == sequence[0]) | (lengths[receiver] == 0), 0, jnp.maximum(slack, 0))
    moved = jax.random.randint(jax.random.fold_in(own, 4), (count // 2,), 0, 1 << 20) % (slack + 1)
    lengths = lengths.at[source_of].add(-moved).at[receiver].add(moved)
    labels = jnp.searchsorted(jnp.cumsum(lengths), jnp.arange(rows * top), side="right").astype(jnp.int32)
    grid = labels.reshape(top, rows).T
    grid = grid[jax.random.permutation(jax.random.fold_in(own, 1), rows)]
    rotation = jax.random.randint(jax.random.fold_in(own, 2), (rows, 1), 0, top)
    return jnp.take_along_axis(grid, (jnp.arange(top)[None, :] + rotation) % top, axis=1)


def shares(number_of, total, reach, lean, full):
    loads = [(1 << 20) // math.isqrt(rank ** lean) + 1 for rank in range(1, number_of + 1)]
    largest = reach if full else min(reach, max(-(-total // number_of), total * loads[0] // sum(loads)))
    least = 1 if total - largest >= number_of - 1 else 0
    given, surplus = [largest] + [least] * (number_of - 1), total - largest - least * (number_of - 1)
    while surplus > 0:
        candidates = [i for i in range(1, number_of) if given[i] < largest] or [i for i in range(1, number_of) if given[i] < reach]
        whole, budget = sum([loads[i] for i in candidates]), surplus
        for i in candidates:
            addition = min(reach - given[i], max(1, budget * loads[i] // whole), surplus)
            given[i] = given[i] + addition
            surplus = surplus - addition
    return np.array(given)


def gaussian(stream_key, extent, deviation, limit, shards=(), kind=jnp.bfloat16):
    values = jax.random.normal(stream_key, extent, jnp.float32) * deviation
    if len(shards) > 0:
        values = levels(stream_key, extent, shards, -0.22, 0.18) * values
    return jnp.clip(values, min=-limit, max=limit).astype(kind)


def bell_draw_with(key, extent, deviation, bound, cuts, heavy, kind=jnp.bfloat16):
    array = deviation * jax.random.normal(key, extent, jnp.float32)
    if cuts:
        array = array * levels(key, extent, cuts, -0.22, 0.18)
    return jnp.clip(raised(array, jax.random.fold_in(key, 3), *heavy), -bound, bound).astype(kind)


def setup_inputs(seed: int = 0) -> dict:
    splits = jax.random.split(jax.random.key(seed), 8)
    teacher_query = draw_teacher_query(jax.random.fold_in(splits[7], 71), 0)
    teacher_keyval = draw_teacher_keyval(jax.random.fold_in(splits[7], 71), 0)
    segment_ids = jnp.searchsorted(jnp.cumsum(uneven_parts(splits[2], DOCS, TOKENS, LONGEST, 1)), jnp.arange(TOKENS), side="right").astype(jnp.int32)
    projector = gaussian(splits[3], (DT, DS), (DT // 64) ** -0.5, 0.5, ((0, 8),))
    owner_table_keys = jax.random.split(jax.random.fold_in(splits[4], 1), TOKENS // TOK_DEV)
    owner_table_turns = jax.random.permutation(jax.random.fold_in(splits[4], 3), TOKENS // TOK_DEV)
    owner_table = jax.vmap(lambda own, number: shared_out(jax.random.fold_in(splits[4], 2), own, number, TOK_DEV, N_SEQ, 1, CAP, 1))(owner_table_keys, owner_table_turns).reshape((TOKENS, 1))
    student_context = bell_draw_with(splits[5], (N_SEQ * SLOTS, DS), 1.0, 6.0, ((0, 16),), (0, 1, 16, 2.0))
    student_out_weight = gaussian(splits[6], (DS, DS), DS ** -0.5, 0.09375, ((0, 16), (1, 8)))
    return {"teacher_query": teacher_query, "teacher_keyval": teacher_keyval, "segment_ids": segment_ids, "projector": projector, "owner_table": owner_table, "student_context": student_context, "student_out_weight": student_out_weight}


def reference(teacher_query, teacher_keyval, segment_ids, projector, owner_table, student_context, student_out_weight):
    per_group = HT // KVT
    query_matrix = teacher_query[0].reshape(TOKENS, HT, HD)
    key_value = teacher_keyval[0].reshape(TOKENS, KVT, 2, HD)
    all_keys = key_value[:, :, 0]
    all_values = key_value[:, :, 1]
    positions = jnp.arange(TOKENS, dtype=jnp.int32)
    allowed = (positions[None, :] <= positions[:, None]) & (segment_ids[None, :] == segment_ids[:, None])
    scaling = HD ** -0.5

    def one_head(head):
        group_index = head // per_group
        head_query = lax.dynamic_index_in_dim(query_matrix, head, 1, keepdims=False)
        per_head_keys = lax.dynamic_index_in_dim(all_keys, group_index, 1, keepdims=False)
        head_values = lax.dynamic_index_in_dim(all_values, group_index, 1, keepdims=False)
        scores = jnp.dot(head_query, per_head_keys.T, preferred_element_type=jnp.float32) * scaling
        row_top = jnp.max(jnp.where(allowed, scores, -1e30), axis=1)
        weights = jnp.where(allowed, jnp.exp(scores - row_top[:, None]), 0.0)
        totals = jnp.sum(weights, axis=1)
        mixed = jnp.dot(weights.astype(jnp.bfloat16), head_values, preferred_element_type=jnp.float32)
        return (mixed / totals[:, None]).astype(jnp.bfloat16)

    context = lax.map(one_head, jnp.arange(HT, dtype=jnp.int32))
    context = jnp.transpose(context, (1, 0, 2)).reshape(TOKENS, HT * HD)
    target = jnp.dot(context, projector, preferred_element_type=jnp.float32).astype(jnp.bfloat16)

    owners = owner_table[:, 0].astype(jnp.int32)
    shard = positions // TOK_DEV
    onehot = (owners[:, None] == jnp.arange(N_SEQ, dtype=jnp.int32)[None, :]).astype(jnp.int32)
    blocked = onehot.reshape(N_SEQ, TOK_DEV, N_SEQ)
    ranking = (jnp.cumsum(blocked, axis=1) - blocked).reshape(TOKENS, N_SEQ)
    ranking = jnp.sum(ranking * onehot, axis=1).astype(jnp.int32)
    slot_index = (owners * SLOTS + shard * CAP + ranking).astype(jnp.int32)
    destination_slots = jnp.zeros((N_SEQ * SLOTS, DS), jnp.bfloat16).at[slot_index].set(target)
    live = jnp.zeros((N_SEQ * SLOTS,), jnp.float32).at[slot_index].set(1.0)

    student_out = jnp.dot(student_context, student_out_weight, preferred_element_type=jnp.float32)
    residual = ((student_out - destination_slots.astype(jnp.float32)) * live[:, None] / TOK_DEV).astype(jnp.bfloat16)
    gradient = jnp.dot(student_context.T, residual, preferred_element_type=jnp.float32)
    return jnp.stack([jnp.zeros_like(gradient), gradient])
```

```python
import functools

import jax
import jax.numpy as jnp
from jax import lax
from jax.experimental import pallas as pl
from jax.experimental.pallas import tpu as pltpu
from jax.sharding import PartitionSpec as P

HD = 128
ZN = 8
WINDOW = 9
PIECE = 272
LOW = -1e30


def ring_pairs(step, base, reps):
    return [
        (base + rep * ZN + z, base + rep * ZN + (z + step) % ZN)
        for rep in range(reps)
        for z in range(ZN)
    ]


def partner_pairs(base):
    return [(base + i, base + (i + ZN) % (2 * ZN)) for i in range(2 * ZN)]


def attention_kernel(info, query, seg_query, pieces, out, acc, top):
    shard = info[0]
    teacher = info[1]
    tok = query.shape[0]
    heads = query.shape[1] // HD
    high = shard // ZN
    ring = lax.rem(shard, ZN)
    scale = (HD**-0.5) * 1.4426950408889634
    count = pieces.shape[0] // PIECE
    seg_q = seg_query[...]
    first_seg = seg_q[0:1, :][0, 0]

    @pl.when(teacher == 0)
    def _():
        top[...] = jnp.full_like(top, LOW)
        acc[...] = jnp.zeros_like(acc)

        def one_block(index, carry):
            pair = index // 2
            other = lax.rem(index, 2)
            dist = (pair + 1) // 2
            sign = 1 - 2 * lax.rem(pair, 2)
            source = lax.rem(ring + sign * dist + ZN, ZN)
            block = (high + other - 2 * high * other) * ZN + source
            start = pl.multiple_of(index * PIECE, 16)
            seg_k = pieces[pl.ds(start + 256, 16), :][0:1, :].astype(jnp.float32)
            last_seg = seg_k[:, 255:256][0, 0]

            @pl.when((block <= shard) & (block >= shard - WINDOW) & (last_seg >= first_seg))
            def _():
                keys = pieces[pl.ds(start, 256), 0:HD]
                values = pieces[pl.ds(start, 256), HD : 2 * HD]
                values = jnp.concatenate([values, jnp.ones_like(values)], axis=1)
                rows = lax.broadcasted_iota(jnp.int32, (tok, 256), 0) + shard * tok
                cols = lax.broadcasted_iota(jnp.int32, (tok, 256), 1) + block * 256
                allowed = (seg_k == seg_q) & (cols <= rows)

                def one_head(head, carry):
                    lanes = pl.ds(pl.multiple_of(head * HD, HD), HD)
                    scores = lax.dot_general(
                        query[:, lanes],
                        keys,
                        (((1,), (1,)), ((), ())),
                        preferred_element_type=jnp.float32,
                    )
                    scores = jnp.where(allowed, scores, LOW)
                    old = top[head]
                    new = jnp.maximum(old, jnp.max(scores, axis=1, keepdims=True))
                    weights = jnp.exp2((scores - new) * scale)
                    fade = jnp.exp2((old - new) * scale)
                    top[head] = new
                    acc[head] = acc[head] * fade + jnp.dot(
                        weights.astype(jnp.bfloat16), values, preferred_element_type=jnp.float32
                    )
                    return carry

                lax.fori_loop(0, heads, one_head, 0, unroll=2)

            return carry

        lax.fori_loop(0, count, one_block, 0)
        for head in range(heads):
            mixed = acc[head]
            out[:, head * HD : (head + 1) * HD] = (mixed[:, :HD] / mixed[:, HD:]).astype(
                jnp.bfloat16
            )


def attend(info, query, seg_query, pieces):
    tok, width = query.shape
    heads = width // HD
    return pl.pallas_call(
        attention_kernel,
        out_shape=jax.ShapeDtypeStruct((tok, width), jnp.bfloat16),
        in_specs=[
            pl.BlockSpec(memory_space=pltpu.SMEM),
            pl.BlockSpec(memory_space=pltpu.VMEM),
            pl.BlockSpec(memory_space=pltpu.VMEM),
            pl.BlockSpec(memory_space=pltpu.VMEM),
        ],
        out_specs=pl.BlockSpec(memory_space=pltpu.VMEM),
        scratch_shapes=[
            pltpu.VMEM((heads, tok, 2 * HD), jnp.float32),
            pltpu.VMEM((heads, tok, 1), jnp.float32),
        ],
        compiler_params=pltpu.CompilerParams(vmem_limit_bytes=32 * 1024 * 1024),
        cost_estimate=pl.CostEstimate(
            flops=8 * tok * width * 2560, bytes_accessed=4 << 20, transcendentals=tok * 8 * 2560
        ),
        name="attend",
    )(info, query, seg_query, pieces)


def gather_keyval(keyval, segments):
    both = ("group", "seq")
    seg_row = jnp.broadcast_to(segments.astype(jnp.bfloat16)[None, :], (16, segments.shape[0]))
    own = jnp.concatenate([keyval, seg_row], axis=0)
    lower = lax.ppermute(own, both, [(z, ZN + z) for z in range(ZN)])
    pair = jnp.concatenate([own, lower], axis=0)
    forward = backward = pair
    found = [pair]
    for _ in range(3):
        forward = lax.ppermute(forward, both, ring_pairs(1, 0, 2))
        backward = lax.ppermute(backward, both, ring_pairs(-1, 0, 2))
        found += [forward, backward]
    found.append(lax.ppermute(forward[:PIECE], both, ring_pairs(1, 0, 2)))
    found.append(lax.ppermute(backward[PIECE:], both, ring_pairs(-1, 0, 2)))
    return jnp.concatenate(found, axis=0)


def shards(
    teacher_query,
    teacher_keyval,
    segment_ids,
    projector,
    owner_table,
    student_context,
    student_out_weight,
):
    group = lax.axis_index("group")
    seq = lax.axis_index("seq")
    high = seq // ZN
    ring = seq % ZN
    query = teacher_query[0]
    tok = query.shape[0]
    slots, model = student_context.shape
    owners_n = 2 * ZN
    capacity = slots // owners_n
    half = model // 2
    feats = student_out_weight.shape[1] // 2
    tensor_n = model // (2 * feats)
    z_groups = [[h * ZN + z for z in range(ZN)] for h in range(2)]

    weight = lax.dynamic_slice_in_dim(student_out_weight, group * feats, feats, axis=1)
    weight = lax.all_gather(weight, "seq", axis=0, tiled=True, axis_index_groups=z_groups)

    pieces = gather_keyval(teacher_keyval[0], segment_ids)

    sent = lax.dynamic_slice_in_dim(
        student_context, (1 - high) * half + group * (half // 2), half // 2, axis=1
    )
    core_swap = [(0, 1), (1, 0)]
    all_pairs = partner_pairs(0) + partner_pairs(owners_n)
    came = lax.ppermute(sent, ("group", "seq"), all_pairs)
    came_other = lax.ppermute(came, "group", core_swap)
    theirs = jnp.where(
        group == 0,
        jnp.concatenate([came, came_other], axis=1),
        jnp.concatenate([came_other, came], axis=1),
    )
    ours = lax.dynamic_slice_in_dim(student_context, high * half, half, axis=1)
    ours = ours.reshape(owners_n, capacity, half)
    theirs = theirs.reshape(owners_n, capacity, half)
    rows = jnp.where(
        high == 0,
        jnp.concatenate([ours, theirs], axis=1),
        jnp.concatenate([theirs, ours], axis=1),
    ).reshape(2 * slots, half)

    info = jnp.stack([seq, group]).astype(jnp.int32)
    seg_query = segment_ids.astype(jnp.float32)[:, None]
    context = attend(info, query, seg_query, pieces)
    passed = lax.ppermute(context, "group", [(0, 1)])
    context = jnp.where(group == 0, context, passed)

    own_projector = lax.dynamic_index_in_dim(
        projector.reshape(projector.shape[0], tensor_n, 2, feats), group, axis=2, keepdims=False
    )
    partial = lax.dot_general(
        context, own_projector, (((1,), (0,)), ((), ())), preferred_element_type=jnp.float32
    ).astype(jnp.bfloat16)
    partial = jnp.transpose(partial, (1, 0, 2))
    partial = lax.all_to_all(partial, "tensor", split_axis=0, concat_axis=0, tiled=True)
    target = jnp.sum(partial.astype(jnp.float32), axis=0).astype(jnp.bfloat16)

    owners_all = owner_table[:, 0]
    owners = lax.dynamic_slice_in_dim(owners_all, seq * tok, tok)
    index = jnp.arange(tok, dtype=jnp.int32)
    ranks = jnp.sum(
        ((owners[:, None] == owners[None, :]) & (index[None, :] < index[:, None])).astype(
            jnp.int32
        ),
        axis=1,
    )
    place = (owners % ZN) * (2 * capacity) + (owners // ZN) * capacity + ranks
    route = (jnp.arange(slots, dtype=jnp.int32)[:, None] == place[None, :]).astype(jnp.bfloat16)
    routed = jnp.dot(route, target, preferred_element_type=jnp.float32).astype(jnp.bfloat16)
    routed = routed.reshape(ZN, 2 * capacity, feats)
    routed = lax.all_to_all(
        jnp.concatenate([routed, routed], axis=0), "seq", split_axis=0, concat_axis=0, tiled=True
    ).reshape(2 * slots, feats)

    output = jnp.dot(rows, weight, preferred_element_type=jnp.float32)
    output = output + lax.ppermute(
        output.astype(jnp.bfloat16), ("group", "seq"), all_pairs
    ).astype(jnp.float32)

    pair_owners = jnp.stack([ring, ring + ZN])
    counts = jnp.sum(
        (owners_all.reshape(owners_n, tok, 1) == pair_owners[None, None, :]).astype(jnp.int32),
        axis=1,
    )
    live = (jnp.arange(capacity, dtype=jnp.int32)[None, None, :] < counts[:, :, None]).reshape(
        2 * slots
    )
    scale = live.astype(jnp.float32)[:, None] / tok
    residual = ((output - routed.astype(jnp.float32)) * scale).astype(jnp.bfloat16)

    gradient = lax.dot_general(
        rows, residual, (((0,), (0,)), ((), ())), preferred_element_type=jnp.float32
    ).astype(jnp.bfloat16)
    gradient = lax.all_to_all(
        gradient.reshape(ZN, half // ZN, feats),
        "seq",
        split_axis=0,
        concat_axis=0,
        tiled=True,
        axis_index_groups=z_groups,
    )
    gradient = jnp.sum(gradient.astype(jnp.float32), axis=0)
    passed = lax.ppermute(gradient, "group", [(0, 1)])
    whole = jnp.concatenate([passed, gradient], axis=1)
    return jnp.where(group == 1, whole, 0.0)[None]


def solution(mesh):
    placed = (
        P("group", "seq", "tensor"),
        P("group", "seq", "tensor"),
        P("seq"),
        P("tensor", None),
        P(),
        P("seq", None),
        P("seq", "tensor"),
    )
    return jax.shard_map(
        shards, mesh=mesh, in_specs=placed, out_specs=P("group", "seq", "tensor"), check_vma=False
    )
```

```python
import functools

import jax
import jax.numpy as jnp
from jax import lax
from jax.experimental import pallas as pl
from jax.experimental.pallas import tpu as pltpu
from jax.sharding import PartitionSpec as P

HD = 128
ZN = 8
WINDOW = 9
PIECE = 272
LOW = -1e30


def ring_pairs(step, base, reps):
    return [
        (base + rep * ZN + z, base + rep * ZN + (z + step) % ZN)
        for rep in range(reps)
        for z in range(ZN)
    ]


def partner_pairs(base):
    return [(base + i, base + (i + ZN) % (2 * ZN)) for i in range(2 * ZN)]


def attention_kernel(info, query, seg_query, *refs):
    parts = refs[:9]
    out, kept, ids, scores, acc, top = refs[9:]
    shard = info[0]
    core = info[1]
    tok = query.shape[0]
    heads = query.shape[1] // HD
    high = shard // ZN
    ring = lax.rem(shard, ZN)
    scale = (HD**-0.5) * 1.4426950408889634
    seg_q = seg_query[...]
    first_seg = seg_q[0:1, :][0, 0]
    away = 1 - 2 * core

    count = jnp.int32(0)
    for index in range(16):
        place = index // 2 if index < 14 else index - 7
        ref = parts[place]
        start = (index % 2) * PIECE if index < 14 else 0
        dist = (place + 1) // 2 if index < 14 else 4
        if index < 14:
            other = jnp.int32(index % 2)
            step = -dist * away if place % 2 == 1 else dist * away
        else:
            other = core if index == 14 else 1 - core
            step = 4
        source = lax.rem(ring + step + ZN, ZN)
        block = (high + other - 2 * high * other) * ZN + source
        last_seg = ref[start + 256 : start + 272, 128:256].astype(jnp.float32)[0:1, 127:128][0, 0]
        wanted = (block <= shard) & (block >= shard - WINDOW) & (last_seg >= first_seg)

        @pl.when(wanted)
        def _(ref=ref, start=start, block=block, count=count):
            kept[count] = ref[start : start + PIECE, :]
            ids[count] = block

        count = count + wanted.astype(jnp.int32)

    top[...] = jnp.full_like(top, LOW)
    acc[...] = jnp.zeros_like(acc)

    def score_block(index, carry):
        keys = kept[index, 0:256, 0:HD]
        seg_k = kept[index, 256:272, :].astype(jnp.float32)[0:1, :]
        rows = lax.broadcasted_iota(jnp.int32, (tok, 256), 0) + shard * tok
        cols = lax.broadcasted_iota(jnp.int32, (tok, 256), 1) + ids[index] * 256
        allowed = (seg_k == seg_q) & (cols <= rows)
        for head in range(heads):
            found = lax.dot_general(
                query[:, head * HD : (head + 1) * HD],
                keys,
                (((1,), (1,)), ((), ())),
                preferred_element_type=jnp.float32,
            )
            found = jnp.where(allowed, found, LOW)
            scores[index, head] = found
            top[head] = jnp.maximum(top[head], jnp.maximum(found[:, :HD], found[:, HD:]))
        return carry

    lax.fori_loop(0, count, score_block, 0)
    for head in range(heads):
        best = jnp.max(top[head], axis=1, keepdims=True)
        top[head] = jnp.broadcast_to(best, (tok, HD))

    def mix_block(index, carry):
        values = kept[index, 0:256, HD : 2 * HD]
        values = jnp.concatenate([values, jnp.ones_like(values)], axis=1)
        for head in range(heads):
            best = top[head]
            shifted = scores[index, head] - jnp.concatenate([best, best], axis=1)
            weights = jnp.exp2(shifted * scale).astype(jnp.bfloat16)
            acc[head] += jnp.dot(weights, values, preferred_element_type=jnp.float32)
        return carry

    lax.fori_loop(0, count, mix_block, 0)
    for head in range(heads):
        mixed = acc[head]
        out[:, head * HD : (head + 1) * HD] = (mixed[:, :HD] / mixed[:, HD:]).astype(jnp.bfloat16)


def attend(info, query, seg_query, parts):
    tok, width = query.shape
    heads = width // HD
    vmem = pl.BlockSpec(memory_space=pltpu.VMEM)
    return pl.pallas_call(
        attention_kernel,
        out_shape=jax.ShapeDtypeStruct((tok, width), jnp.bfloat16),
        in_specs=[pl.BlockSpec(memory_space=pltpu.SMEM)] + [vmem] * (2 + len(parts)),
        out_specs=vmem,
        scratch_shapes=[
            pltpu.VMEM((16, PIECE, 2 * HD), jnp.bfloat16),
            pltpu.SMEM((16,), jnp.int32),
            pltpu.VMEM((16, heads, tok, 256), jnp.float32),
            pltpu.VMEM((heads, tok, 2 * HD), jnp.float32),
            pltpu.VMEM((heads, tok, HD), jnp.float32),
        ],
        compiler_params=pltpu.CompilerParams(vmem_limit_bytes=40 * 1024 * 1024),
        cost_estimate=pl.CostEstimate(
            flops=8 * tok * width * 2560,
            bytes_accessed=4 << 20,
            transcendentals=tok * heads * 2560,
        ),
        name="attend",
    )(info, query, seg_query, *parts)


def project_kernel(core, context, weight, out):
    out[0] = jnp.dot(context[...], weight[...], preferred_element_type=jnp.float32).astype(
        jnp.bfloat16
    )


def project(core, context, projector, tensor_n):
    tok, width = context.shape
    feats = projector.shape[1] // (2 * tensor_n)
    return pl.pallas_call(
        project_kernel,
        out_shape=jax.ShapeDtypeStruct((tensor_n, tok, feats), jnp.bfloat16),
        grid_spec=pltpu.PrefetchScalarGridSpec(
            num_scalar_prefetch=1,
            grid=(tensor_n,),
            in_specs=[
                pl.BlockSpec((tok, width), lambda i, core: (0, 0)),
                pl.BlockSpec((width, feats), lambda i, core: (0, 2 * i + core[0])),
            ],
            out_specs=pl.BlockSpec((1, tok, feats), lambda i, core: (i, 0, 0)),
        ),
        compiler_params=pltpu.CompilerParams(vmem_limit_bytes=16 * 1024 * 1024),
        cost_estimate=pl.CostEstimate(
            flops=2 * tok * width * feats * tensor_n,
            bytes_accessed=2 * width * feats * tensor_n,
            transcendentals=0,
        ),
        name="project",
    )(core, context, projector)


def gather_keyval(group, keyval, query, segments):
    both = ("group", "seq")
    tok, width = query.shape
    seg_row = jnp.broadcast_to(segments.astype(jnp.bfloat16)[None, :], (16, segments.shape[0]))
    own = jnp.concatenate([keyval, seg_row], axis=0)
    lower = lax.ppermute(own, both, [(z, ZN + z) for z in range(ZN)])
    own = jnp.where(group == 0, own, lax.ppermute(own, "group", [(0, 1)]))
    other_query = lax.ppermute(query[:, width // 2 :], "group", [(0, 1)])
    query = jnp.where(group == 0, query[:, : width // 2], other_query)
    lower = jnp.where(group == 0, lower, lax.ppermute(lower, "group", [(0, 1)]))
    moving = jnp.concatenate([own, lower], axis=0)
    pairs = ring_pairs(1, 0, 2) + ring_pairs(-1, 2 * ZN, 2)
    swap = [(0, 1), (1, 0)]
    found = [moving]
    for _ in range(3):
        moving = lax.ppermute(moving, both, pairs)
        found += [moving, lax.ppermute(moving, "group", swap)]
    moving = jnp.where(group == 0, moving[:PIECE], moving[PIECE:])
    moving = lax.ppermute(moving, both, pairs)
    found += [moving, lax.ppermute(moving, "group", swap)]
    return query, found


def shards(
    teacher_query,
    teacher_keyval,
    segment_ids,
    projector,
    owner_table,
    student_context,
    student_out_weight,
):
    group = lax.axis_index("group")
    seq = lax.axis_index("seq")
    high = seq // ZN
    ring = seq % ZN
    query = teacher_query[0]
    tok = query.shape[0]
    slots, model = student_context.shape
    owners_n = 2 * ZN
    capacity = slots // owners_n
    half = model // 2
    feats = student_out_weight.shape[1] // 2
    tensor_n = model // (2 * feats)
    z_groups = [[h * ZN + z for z in range(ZN)] for h in range(2)]

    weight = lax.dynamic_slice_in_dim(student_out_weight, group * feats, feats, axis=1)
    weight, keyval = lax.optimization_barrier((weight, teacher_keyval[0]))
    weight = lax.all_gather(weight, "seq", axis=0, tiled=True, axis_index_groups=z_groups)

    query, parts = gather_keyval(group, keyval, query, segment_ids)

    sent = lax.dynamic_slice_in_dim(
        student_context, (1 - high) * half + group * (half // 2), half // 2, axis=1
    )
    core_swap = [(0, 1), (1, 0)]
    all_pairs = partner_pairs(0) + partner_pairs(owners_n)
    came = lax.ppermute(sent, ("group", "seq"), all_pairs)
    came_other = lax.ppermute(came, "group", core_swap)
    theirs = jnp.where(
        group == 0,
        jnp.concatenate([came, came_other], axis=1),
        jnp.concatenate([came_other, came], axis=1),
    )
    ours = lax.dynamic_slice_in_dim(student_context, high * half, half, axis=1)
    ours = ours.reshape(owners_n, capacity, half)
    theirs = theirs.reshape(owners_n, capacity, half)
    rows = jnp.where(
        high == 0,
        jnp.concatenate([ours, theirs], axis=1),
        jnp.concatenate([theirs, ours], axis=1),
    ).reshape(2 * slots, half)

    info = jnp.stack([seq, group]).astype(jnp.int32)
    seg_query = segment_ids.astype(jnp.float32)[:, None]
    context = attend(info, query, seg_query, parts)

    owners_all = owner_table[:, 0]
    owners = lax.dynamic_slice_in_dim(owners_all, seq * tok, tok)
    index = jnp.arange(tok, dtype=jnp.int32)
    ranks = jnp.sum(
        ((owners[:, None] == owners[None, :]) & (index[None, :] < index[:, None])).astype(
            jnp.int32
        ),
        axis=1,
    )
    place = (owners % ZN) * (2 * capacity) + (owners // ZN) * capacity + ranks
    route = (jnp.arange(slots, dtype=jnp.int32)[:, None] == place[None, :]).astype(jnp.bfloat16)
    pair_owners = jnp.stack([ring, ring + ZN])
    counts = jnp.sum(
        (owners_all.reshape(owners_n, tok, 1) == pair_owners[None, None, :]).astype(jnp.int32),
        axis=1,
    )
    live = (jnp.arange(capacity, dtype=jnp.int32)[None, None, :] < counts[:, :, None]).reshape(
        2 * slots
    )
    scale = live.astype(jnp.float32)[:, None] / tok
    context, route, scale = lax.optimization_barrier((context, route, scale))

    other_context = lax.ppermute(context, "group", core_swap)
    context = jnp.where(
        group == 0,
        jnp.concatenate([context, other_context], axis=1),
        jnp.concatenate([other_context, context], axis=1),
    )
    partial = project(group[None].astype(jnp.int32), context, projector, tensor_n)
    partial = lax.all_to_all(partial, "tensor", split_axis=0, concat_axis=0, tiled=True)
    target = jnp.sum(partial.astype(jnp.float32), axis=0).astype(jnp.bfloat16)

    output = jnp.dot(rows, weight, preferred_element_type=jnp.float32)
    output = output + lax.ppermute(
        output.astype(jnp.bfloat16), ("group", "seq"), all_pairs
    ).astype(jnp.float32)

    output, target = lax.optimization_barrier((output, target))

    routed = jnp.dot(route, target, preferred_element_type=jnp.float32).astype(jnp.bfloat16)
    routed = routed.reshape(ZN, 2 * capacity, feats)
    routed = lax.all_to_all(
        jnp.concatenate([routed, routed], axis=0), "seq", split_axis=0, concat_axis=0, tiled=True
    ).reshape(2 * slots, feats)

    residual = ((output - routed.astype(jnp.float32)) * scale).astype(jnp.bfloat16)

    gradient = lax.dot_general(
        rows, residual, (((0,), (0,)), ((), ())), preferred_element_type=jnp.float32
    ).astype(jnp.bfloat16)
    gradient = lax.all_to_all(
        gradient.reshape(ZN, half // ZN, feats),
        "seq",
        split_axis=0,
        concat_axis=0,
        tiled=True,
        axis_index_groups=z_groups,
    )
    gradient = jnp.sum(gradient.astype(jnp.float32), axis=0)
    passed = lax.ppermute(gradient, "group", [(0, 1)])
    whole = jnp.concatenate([passed, gradient], axis=1)
    return jnp.where(group == 1, whole, 0.0)[None]


def solution(mesh):
    placed = (
        P("group", "seq", "tensor"),
        P("group", "seq", "tensor"),
        P("seq"),
        P("tensor", None),
        P(),
        P("seq", None),
        P("seq", "tensor"),
    )
    return jax.shard_map(
        shards, mesh=mesh, in_specs=placed, out_specs=P("group", "seq", "tensor"), check_vma=False
    )
```

```python
import functools

import jax
import jax.numpy as jnp
from jax import lax
from jax.experimental import pallas as pl
from jax.experimental.pallas import tpu as pltpu
from jax.sharding import PartitionSpec as P

HD = 128
ZN = 8
WINDOW = 9
PIECE = 272
LOW = -1e30


def along_x(step):
    return [(2 * x + y, 2 * ((x + step) % 4) + y) for x in range(4) for y in range(2)]


def partner_pairs(base):
    return [(base + i, base + (i + ZN) % (2 * ZN)) for i in range(2 * ZN)]


def attention_kernel(
    info, query, seg_query, mine, other, out, kept, seg_kept, stacked, scores, acc, top
):
    shard = info[0]
    core = info[1]
    tok = query.shape[0]
    heads = query.shape[1] // HD
    scale = (HD**-0.5) * 1.4426950408889634
    seg_q = seg_query[...]
    first_seg = seg_q[0:1, :][0, 0]

    def keep_block(block, count):
        tail = mine[block, 256:272, :].astype(jnp.float32)
        last_seg = tail[1:2, HD - 1 : HD][0, 0]
        wanted = (block >= shard - WINDOW) & (last_seg >= first_seg)

        @pl.when(wanted)
        def _():
            first = mine[block, 0:256, :]
            second = other[block, 0:256, :]
            rows = pl.ds(pl.multiple_of(count * 256, 256), 256)
            kept[rows, 0:HD] = jnp.where(core == 0, first, second)
            kept[rows, HD : 2 * HD] = jnp.where(core == 0, second, first)
            seg_kept[count] = jnp.concatenate([tail[0:1, :], tail[1:2, :]], axis=1)

        return count + wanted.astype(jnp.int32)

    count = lax.fori_loop(0, shard + 1, keep_block, jnp.int32(0))

    @pl.when(lax.rem(count, 2) == 1)
    def _():
        kept[pl.ds(pl.multiple_of(count * 256, 256), 256), :] = jnp.zeros(
            (256, 2 * HD), jnp.bfloat16
        )
        seg_kept[count] = jnp.full((1, 256), -1.0, jnp.float32)

    for head in range(heads):
        stacked[head * tok : (head + 1) * tok, :] = query[:, head * HD : (head + 1) * HD]
    top[...] = jnp.full_like(top, LOW)
    acc[...] = jnp.zeros_like(acc)
    causal = lax.broadcasted_iota(jnp.int32, (tok, 256), 1) <= lax.broadcasted_iota(
        jnp.int32, (tok, 256), 0
    )

    def score_pair(pair, carry):
        keys = kept[pl.ds(pl.multiple_of(pair * 512, 512), 512), 0:HD]
        found = lax.dot_general(
            stacked[...], keys, (((1,), (1,)), ((), ())), preferred_element_type=jnp.float32
        )
        for side in range(2):
            index = 2 * pair + side
            allowed = (seg_kept[index] == seg_q) & (causal | (index != count - 1))
            for head in range(heads):
                rows = slice(head * tok, (head + 1) * tok)
                part = jnp.where(allowed, found[rows, side * 256 : (side + 1) * 256], LOW)
                scores[index, rows, :] = part
                top[rows, :] = jnp.maximum(top[rows, :], jnp.maximum(part[:, :HD], part[:, HD:]))
        return carry

    pairs = (count + 1) // 2
    lax.fori_loop(0, pairs, score_pair, 0)
    top[...] = jnp.broadcast_to(jnp.max(top[...], axis=1, keepdims=True), top.shape)

    def mix_pair(pair, carry):
        values = kept[pl.ds(pl.multiple_of(pair * 512, 512), 512), HD : 2 * HD]
        values = jnp.concatenate([values, jnp.ones_like(values)], axis=1)
        best = jnp.concatenate([top[...], top[...]], axis=1)
        weights = jnp.concatenate(
            [
                jnp.exp2((scores[2 * pair + side] - best) * scale).astype(jnp.bfloat16)
                for side in range(2)
            ],
            axis=1,
        )
        acc[...] += jnp.dot(weights, values, preferred_element_type=jnp.float32)
        return carry

    lax.fori_loop(0, pairs, mix_pair, 0)
    for head in range(heads):
        mixed = acc[head * tok : (head + 1) * tok, :]
        out[:, head * HD : (head + 1) * HD] = (mixed[:, :HD] / mixed[:, HD:]).astype(jnp.bfloat16)


def attend(info, query, seg_query, mine, other):
    tok, width = query.shape
    heads = width // HD
    blocks = WINDOW + 1
    vmem = pl.BlockSpec(memory_space=pltpu.VMEM)
    return pl.pallas_call(
        attention_kernel,
        out_shape=jax.ShapeDtypeStruct((tok, width), jnp.bfloat16),
        in_specs=[pl.BlockSpec(memory_space=pltpu.SMEM)] + [vmem] * 4,
        out_specs=vmem,
        scratch_shapes=[
            pltpu.VMEM((blocks * 256, 2 * HD), jnp.bfloat16),
            pltpu.VMEM((blocks, 1, 256), jnp.float32),
            pltpu.VMEM((heads * tok, HD), jnp.bfloat16),
            pltpu.VMEM((blocks, heads * tok, 256), jnp.float32),
            pltpu.VMEM((heads * tok, 2 * HD), jnp.float32),
            pltpu.VMEM((heads * tok, HD), jnp.float32),
        ],
        compiler_params=pltpu.CompilerParams(vmem_limit_bytes=40 * 1024 * 1024),
        cost_estimate=pl.CostEstimate(
            flops=8 * tok * width * 2560,
            bytes_accessed=4 << 20,
            transcendentals=tok * heads * 2560,
        ),
        name="attend",
    )(info, query, seg_query, mine, other)


def project_kernel(core, context, weight, out):
    out[0] = jnp.dot(context[...], weight[...], preferred_element_type=jnp.float32).astype(
        jnp.bfloat16
    )


def project(core, context, projector, tensor_n):
    tok, width = context.shape
    feats = projector.shape[1] // (2 * tensor_n)
    return pl.pallas_call(
        project_kernel,
        out_shape=jax.ShapeDtypeStruct((tensor_n, tok, feats), jnp.bfloat16),
        grid_spec=pltpu.PrefetchScalarGridSpec(
            num_scalar_prefetch=1,
            grid=(tensor_n,),
            in_specs=[
                pl.BlockSpec((tok, width), lambda i, core: (0, 0)),
                pl.BlockSpec((width, feats), lambda i, core: (0, 2 * i + core[0])),
            ],
            out_specs=pl.BlockSpec((1, tok, feats), lambda i, core: (i, 0, 0)),
        ),
        compiler_params=pltpu.CompilerParams(vmem_limit_bytes=16 * 1024 * 1024),
        cost_estimate=pl.CostEstimate(
            flops=2 * tok * width * feats * tensor_n,
            bytes_accessed=2 * width * feats * tensor_n,
            transcendentals=0,
        ),
        name="project",
    )(core, context, projector)


def student_kernel(place, ours, near, far, weight, out):
    x_place = place[0]
    core = place[1]
    feats = weight.shape[1]
    out[:, 0:feats] = jnp.dot(
        ours[...], weight[...], preferred_element_type=jnp.float32
    ).astype(jnp.bfloat16)
    total = None
    for step in range(4):
        for blocks, side in ((near, core), (far, 1 - core)):
            start = (lax.rem(x_place + step, 4) * 2 + side) * 256
            part = jnp.dot(
                blocks[step],
                weight[pl.ds(pl.multiple_of(start, 256), 256), :],
                preferred_element_type=jnp.float32,
            )
            total = part if total is None else total + part
    out[:, feats:] = total.astype(jnp.bfloat16)


def gradient_kernel(place, ours, near, far, output, theirs, routed, scale, out):
    x_place = place[0]
    core = place[1]
    feats = output.shape[1] // 2

    def residual(lanes, other_lanes, column):
        whole = output[:, lanes].astype(jnp.float32) + theirs[:, other_lanes].astype(jnp.float32)
        whole = whole - routed[:, lanes].astype(jnp.float32)
        return (whole * scale[:, column : column + 1]).astype(jnp.bfloat16)

    left, right = slice(0, feats), slice(feats, 2 * feats)
    own = residual(left, right, 0)
    partner = residual(right, left, 1)
    over_rows = (((0,), (0,)), ((), ()))
    for step in range(4):
        for blocks, side in ((near, core), (far, 1 - core)):
            index = lax.rem(x_place + step, 4) * 2 + side
            columns = pl.ds(pl.multiple_of(index * 256, 256), 256)
            out[index] = (
                lax.dot_general(
                    ours[:, columns], own, over_rows, preferred_element_type=jnp.float32
                )
                + lax.dot_general(
                    blocks[step], partner, over_rows, preferred_element_type=jnp.float32
                )
            ).astype(jnp.bfloat16)


def on_core(kernel, name, shape, flops, place, *args):
    vmem = pl.BlockSpec(memory_space=pltpu.VMEM)
    return pl.pallas_call(
        kernel,
        out_shape=jax.ShapeDtypeStruct(shape, jnp.bfloat16),
        in_specs=[pl.BlockSpec(memory_space=pltpu.SMEM)] + [vmem] * len(args),
        out_specs=vmem,
        compiler_params=pltpu.CompilerParams(vmem_limit_bytes=32 * 1024 * 1024),
        cost_estimate=pl.CostEstimate(flops=flops, bytes_accessed=6 << 20, transcendentals=0),
        name=name,
    )(place, *args)


def gather_keyval(group, keyval, query, segments, rest):
    tok, width = query.shape
    swap = [(0, 1), (1, 0)]
    seg_rows = segments.astype(jnp.bfloat16).reshape(2, HD)
    seg_rows = jnp.concatenate([seg_rows, jnp.zeros((14, HD), jnp.bfloat16)], axis=0)
    passed = lax.ppermute(keyval, "group", [(0, 1)])
    piece = jnp.where(group == 0, keyval[:, :HD], passed[:, HD:])
    piece = jnp.concatenate([piece, seg_rows], axis=0)
    pieces = jnp.broadcast_to(piece[None], (2 * ZN, PIECE, HD))
    pieces, query = lax.optimization_barrier((pieces, query))
    mine = lax.all_to_all(pieces, "seq", split_axis=0, concat_axis=0, tiled=True)
    other = lax.ppermute(mine, "group", swap)
    after = lax.ppermute(mine[0, :16], "group", swap)
    other_query = lax.ppermute(query[:, width // 2 :], "group", [(0, 1)])
    other_query, rest = lax.optimization_barrier((other_query, rest))
    query = jnp.where(group == 0, query[:, : width // 2], other_query)
    return query, mine, other, after, rest


def shards(
    teacher_query,
    teacher_keyval,
    segment_ids,
    projector,
    owner_table,
    student_context,
    student_out_weight,
):
    group = lax.axis_index("group")
    seq = lax.axis_index("seq")
    high = seq // ZN
    query = teacher_query[0]
    tok = query.shape[0]
    slots, model = student_context.shape
    owners_n = 2 * ZN
    capacity = slots // owners_n
    half = model // 2
    feats = student_out_weight.shape[1] // 2
    tensor_n = model // (2 * feats)
    z_groups = [[h * ZN + z for z in range(ZN)] for h in range(2)]

    query, mine, other, after, (student_context, student_out_weight, owner_table) = gather_keyval(
        group,
        teacher_keyval[0],
        query,
        segment_ids,
        (student_context, student_out_weight, owner_table),
    )
    weight = lax.dynamic_slice_in_dim(student_out_weight, group * feats, feats, axis=1)
    weight = jnp.broadcast_to(weight[None], (ZN,) + weight.shape)
    weight, after = lax.optimization_barrier((weight, after))
    weight = lax.all_to_all(
        weight, "seq", split_axis=0, concat_axis=0, tiled=True, axis_index_groups=z_groups
    ).reshape(half, feats)

    core_swap = [(0, 1), (1, 0)]
    all_pairs = partner_pairs(0) + partner_pairs(owners_n)
    quarter = half // 4
    x_place = lax.axis_index("tensor") // 2
    sent = lax.dynamic_slice_in_dim(
        student_context,
        (1 - high) * half + x_place * quarter + group * (quarter // 2),
        quarter // 2,
        axis=1,
    )
    came = lax.ppermute(sent, ("group", "seq"), all_pairs)
    behind = lax.ppermute(came, "tensor", along_x(1))
    ahead = lax.ppermute(came, "tensor", along_x(-1))
    across = lax.ppermute(came, "tensor", along_x(2))
    near = jnp.stack([came, ahead, across, behind])
    far = lax.ppermute(near, "group", core_swap)
    ours = lax.dynamic_slice_in_dim(student_context, high * half, half, axis=1)
    place = jnp.stack([x_place, group]).astype(jnp.int32)

    info = jnp.stack([seq, group]).astype(jnp.int32)
    seg_query = segment_ids.astype(jnp.float32)[:, None]

    owners_all = owner_table[:, 0]
    owners = lax.dynamic_slice_in_dim(owners_all, seq * tok, tok)
    index = jnp.arange(tok, dtype=jnp.int32)
    ranks = jnp.sum(
        ((owners[:, None] == owners[None, :]) & (index[None, :] < index[:, None])).astype(
            jnp.int32
        ),
        axis=1,
    )
    slot = owners * capacity + ranks
    route = (jnp.arange(slots, dtype=jnp.int32)[:, None] == slot[None, :]).astype(jnp.bfloat16)
    pair_owners = jnp.stack([seq, (seq + ZN) % owners_n])
    counts = jnp.sum(
        (owners_all.reshape(owners_n, tok, 1) == pair_owners[None, None, :]).astype(jnp.int32),
        axis=1,
    )
    live = jnp.arange(capacity, dtype=jnp.int32)[None, :, None] < counts[:, None, :]
    scale = live.reshape(slots, 2).astype(jnp.float32) / tok
    mine, route, scale, near, far, ours = lax.optimization_barrier(
        (mine, route, scale, near, far, ours)
    )
    context = attend(info, query, seg_query, mine, other)

    other_context = lax.ppermute(context, "group", core_swap)
    context = jnp.where(
        group == 0,
        jnp.concatenate([context, other_context], axis=1),
        jnp.concatenate([other_context, context], axis=1),
    )
    partial = project(group[None].astype(jnp.int32), context, projector, tensor_n)
    partial = lax.all_to_all(partial, "tensor", split_axis=0, concat_axis=0, tiled=True)
    output = on_core(
        student_kernel, "student", (slots, 2 * feats), 4 * slots * half * feats,
        place, ours, near, far, weight,
    )
    partial, output = lax.optimization_barrier((partial, output))
    theirs = lax.ppermute(output, ("group", "seq"), all_pairs)
    target = jnp.sum(partial.astype(jnp.float32), axis=0).astype(jnp.bfloat16)

    routed = jnp.dot(route, target, preferred_element_type=jnp.float32).astype(jnp.bfloat16)
    routed = jnp.concatenate([routed, jnp.roll(routed, slots // 2, axis=0)], axis=1)
    routed = lax.all_to_all(
        routed.reshape(owners_n, capacity, 2 * feats),
        "seq",
        split_axis=0,
        concat_axis=0,
        tiled=True,
    ).reshape(slots, 2 * feats)

    gradient = on_core(
        gradient_kernel, "gradient", (ZN, half // ZN, feats), 4 * slots * half * feats,
        place, ours, near, far, output, theirs, routed, scale,
    )
    gradient = lax.all_to_all(
        gradient,
        "seq",
        split_axis=0,
        concat_axis=0,
        tiled=True,
        axis_index_groups=z_groups,
    )
    gradient = jnp.sum(gradient.astype(jnp.float32), axis=0)
    passed = lax.ppermute(gradient, "group", [(0, 1)])
    whole = jnp.concatenate([passed, gradient], axis=1)
    return jnp.where(group == 1, whole, 0.0)[None]


def solution(mesh):
    placed = (
        P("group", "seq", "tensor"),
        P("group", "seq", "tensor"),
        P("seq"),
        P("tensor", None),
        P(),
        P("seq", None),
        P("seq", "tensor"),
    )
    return jax.shard_map(
        shards, mesh=mesh, in_specs=placed, out_specs=P("group", "seq", "tensor"), check_vma=False
    )
```

```python
import functools

import jax
import jax.numpy as jnp
from jax import lax
from jax.experimental import pallas as pl
from jax.experimental.pallas import tpu as pltpu
from jax.sharding import PartitionSpec as P

HD = 128
ZN = 8
WINDOW = 9
PIECE = 272
LOW = -1e30


def partner_pairs(base):
    return [(base + i, base + (i + ZN) % (2 * ZN)) for i in range(2 * ZN)]


def attention_kernel(
    info, query, seg_query, mine, other, out, kept, seg_kept, stacked, scores, acc, top
):
    shard = info[0]
    core = info[1]
    tok = query.shape[0]
    heads = query.shape[1] // HD
    scale = (HD**-0.5) * 1.4426950408889634
    seg_q = seg_query[...]
    first_seg = seg_q[0:1, :][0, 0]

    upper = shard // ZN
    ring = lax.rem(shard, ZN)

    def keep_block(step, count):
        place = lax.rem(ring + 1 + step, ZN)
        place = jnp.where(step < ZN, place, step)
        block = jnp.where(place <= ring, upper * ZN + place, place)
        block = jnp.where(place == ZN, ring, block)
        block = jnp.where(place == ZN + 1, ring - 1, block)
        tail = mine[place, 256:272, :].astype(jnp.float32)
        last_seg = tail[1:2, HD - 1 : HD][0, 0]
        wanted = (block >= 0) & (block >= shard - WINDOW) & (block <= shard)
        wanted = wanted & (last_seg >= first_seg) & ((step < ZN) | (upper == 1))

        @pl.when(wanted)
        def _():
            first = mine[place, 0:256, :]
            second = other[place, 0:256, :]
            rows = pl.ds(pl.multiple_of(count * 256, 256), 256)
            kept[rows, 0:HD] = jnp.where(core == 0, first, second)
            kept[rows, HD : 2 * HD] = jnp.where(core == 0, second, first)
            seg_kept[count] = jnp.concatenate([tail[0:1, :], tail[1:2, :]], axis=1)

        return count + wanted.astype(jnp.int32)

    count = lax.fori_loop(ZN, ZN + 2, keep_block, jnp.int32(0))
    count = lax.fori_loop(0, ZN, keep_block, count)

    @pl.when(lax.rem(count, 2) == 1)
    def _():
        kept[pl.ds(pl.multiple_of(count * 256, 256), 256), :] = jnp.zeros(
            (256, 2 * HD), jnp.bfloat16
        )
        seg_kept[count] = jnp.full((1, 256), -1.0, jnp.float32)

    for head in range(heads):
        stacked[head * tok : (head + 1) * tok, :] = query[:, head * HD : (head + 1) * HD]
    top[...] = jnp.full_like(top, LOW)
    acc[...] = jnp.zeros_like(acc)
    causal = lax.broadcasted_iota(jnp.int32, (tok, 256), 1) <= lax.broadcasted_iota(
        jnp.int32, (tok, 256), 0
    )

    def score_pair(pair, carry):
        keys = kept[pl.ds(pl.multiple_of(pair * 512, 512), 512), 0:HD]
        found = lax.dot_general(
            stacked[...], keys, (((1,), (1,)), ((), ())), preferred_element_type=jnp.float32
        )
        for side in range(2):
            index = 2 * pair + side
            allowed = (seg_kept[index] == seg_q) & (causal | (index != count - 1))
            for head in range(heads):
                rows = slice(head * tok, (head + 1) * tok)
                part = jnp.where(allowed, found[rows, side * 256 : (side + 1) * 256], LOW)
                scores[index, rows, :] = part
                top[rows, :] = jnp.maximum(top[rows, :], jnp.maximum(part[:, :HD], part[:, HD:]))
        return carry

    pairs = (count + 1) // 2
    lax.fori_loop(0, pairs, score_pair, 0)
    top[...] = jnp.broadcast_to(jnp.max(top[...], axis=1, keepdims=True), top.shape)

    def mix_pair(pair, carry):
        values = kept[pl.ds(pl.multiple_of(pair * 512, 512), 512), HD : 2 * HD]
        values = jnp.concatenate([values, jnp.ones_like(values)], axis=1)
        best = jnp.concatenate([top[...], top[...]], axis=1)
        weights = jnp.concatenate(
            [
                jnp.exp2((scores[2 * pair + side] - best) * scale).astype(jnp.bfloat16)
                for side in range(2)
            ],
            axis=1,
        )
        acc[...] += jnp.dot(weights, values, preferred_element_type=jnp.float32)
        return carry

    lax.fori_loop(0, pairs, mix_pair, 0)
    for head in range(heads):
        mixed = acc[head * tok : (head + 1) * tok, :]
        out[:, head * HD : (head + 1) * HD] = (mixed[:, :HD] / mixed[:, HD:]).astype(jnp.bfloat16)


def attend(info, query, seg_query, mine, other):
    tok, width = query.shape
    heads = width // HD
    blocks = WINDOW + 1
    vmem = pl.BlockSpec(memory_space=pltpu.VMEM)
    return pl.pallas_call(
        attention_kernel,
        out_shape=jax.ShapeDtypeStruct((tok, width), jnp.bfloat16),
        in_specs=[pl.BlockSpec(memory_space=pltpu.SMEM)] + [pl.BlockSpec()] * 4,
        out_specs=vmem,
        scratch_shapes=[
            pltpu.VMEM((blocks * 256, 2 * HD), jnp.bfloat16),
            pltpu.VMEM((blocks, 1, 256), jnp.float32),
            pltpu.VMEM((heads * tok, HD), jnp.bfloat16),
            pltpu.VMEM((blocks, heads * tok, 256), jnp.float32),
            pltpu.VMEM((heads * tok, 2 * HD), jnp.float32),
            pltpu.VMEM((heads * tok, HD), jnp.float32),
        ],
        compiler_params=pltpu.CompilerParams(vmem_limit_bytes=24 * 1024 * 1024),
        cost_estimate=pl.CostEstimate(
            flops=8 * tok * width * 2560,
            bytes_accessed=4 << 20,
            transcendentals=tok * heads * 2560,
        ),
        name="attend",
    )(info, query, seg_query, mine, other)


def select_kernel(core, low, high, out):
    out[0] = jnp.concatenate([low[...], high[...]], axis=1)


def select_columns(core, projector, tensor_n):
    width = projector.shape[0]
    lanes = projector.shape[1] // (4 * tensor_n)
    return pl.pallas_call(
        select_kernel,
        out_shape=jax.ShapeDtypeStruct((tensor_n, width, 2 * lanes), projector.dtype),
        grid_spec=pltpu.PrefetchScalarGridSpec(
            num_scalar_prefetch=1,
            grid=(tensor_n,),
            in_specs=[
                pl.BlockSpec((width, lanes), lambda i, core: (0, 4 * i + core[0])),
                pl.BlockSpec((width, lanes), lambda i, core: (0, 4 * i + 2 + core[0])),
            ],
            out_specs=pl.BlockSpec((1, width, 2 * lanes), lambda i, core: (i, 0, 0)),
        ),
        compiler_params=pltpu.CompilerParams(vmem_limit_bytes=48 * 1024 * 1024),
        cost_estimate=pl.CostEstimate(
            flops=0, bytes_accessed=8 * width * lanes * tensor_n, transcendentals=0
        ),
        name="select_columns",
    )(core, projector, projector)


def project_kernel(context, weight, out):
    out[0] = jnp.dot(context[...], weight[0], preferred_element_type=jnp.float32).astype(
        jnp.bfloat16
    )


def project(context, weight):
    tok, width = context.shape
    blocks, _, feats = weight.shape
    return pl.pallas_call(
        project_kernel,
        out_shape=jax.ShapeDtypeStruct((blocks, tok, feats), jnp.bfloat16),
        grid=(blocks,),
        in_specs=[
            pl.BlockSpec((tok, width), lambda i: (0, 0)),
            pl.BlockSpec((1, width, feats), lambda i: (i, 0, 0)),
        ],
        out_specs=pl.BlockSpec((1, tok, feats), lambda i: (i, 0, 0)),
        compiler_params=pltpu.CompilerParams(vmem_limit_bytes=16 * 1024 * 1024),
        cost_estimate=pl.CostEstimate(
            flops=2 * tok * width * feats * blocks,
            bytes_accessed=2 * width * feats * blocks,
            transcendentals=0,
        ),
        name="project",
    )(context, weight)


def student_kernel(place, ours_low, ours_high, theirs_low, theirs_high, weight, kept, sent):
    core = place[1]
    middle = ours_low.shape[1]

    def product(low, high):
        return jnp.dot(
            low[...], weight[:middle, :], preferred_element_type=jnp.float32
        ) + jnp.dot(high[...], weight[middle:, :], preferred_element_type=jnp.float32)

    own = product(ours_low, ours_high)
    partner = product(theirs_low, theirs_high)
    lanes = own.shape[1] // 2
    first = jnp.concatenate([own[:, :lanes], partner[:, :lanes]], axis=1)
    second = jnp.concatenate([own[:, lanes:], partner[:, lanes:]], axis=1)
    kept[...] = jnp.where(core == 0, first, second)
    sent[...] = jnp.where(core == 0, second, first).astype(jnp.bfloat16)


def gradient_kernel(place, ours_low, ours_high, theirs_low, theirs_high, mine, other, out):
    core = place[1]
    lanes = mine.shape[1] // 2
    first = jnp.where(core == 0, mine[...], other[...])
    second = jnp.where(core == 0, other[...], mine[...])
    own = jnp.concatenate([first[:, :lanes], second[:, :lanes]], axis=1)
    partner = jnp.concatenate([first[:, lanes:], second[:, lanes:]], axis=1)
    over_rows = (((0,), (0,)), ((), ()))
    count, width = out.shape[0] // 2, out.shape[1]
    for side, (ours, theirs) in enumerate(((ours_low, theirs_low), (ours_high, theirs_high))):
        for index in range(count):
            columns = slice(index * width, (index + 1) * width)
            out[side * count + index] = (
                lax.dot_general(ours[:, columns], own, over_rows, preferred_element_type=jnp.float32)
                + lax.dot_general(
                    theirs[:, columns], partner, over_rows, preferred_element_type=jnp.float32
                )
            ).astype(jnp.bfloat16)


def on_core(kernel, name, out_shape, flops, place, *args):
    vmem = pl.BlockSpec(memory_space=pltpu.VMEM)
    return pl.pallas_call(
        kernel,
        out_shape=out_shape,
        in_specs=[pl.BlockSpec(memory_space=pltpu.SMEM)] + [vmem] * len(args),
        out_specs=jax.tree.map(lambda _: vmem, out_shape),
        compiler_params=pltpu.CompilerParams(vmem_limit_bytes=32 * 1024 * 1024),
        cost_estimate=pl.CostEstimate(flops=flops, bytes_accessed=6 << 20, transcendentals=0),
        name=name,
    )(place, *args)


def shards(
    teacher_query,
    teacher_keyval,
    segment_ids,
    projector,
    owner_table,
    student_context,
    student_out_weight,
):
    group = lax.axis_index("group")
    seq = lax.axis_index("seq")
    high = seq // ZN
    query = teacher_query[0]
    tok = query.shape[0]
    slots, model = student_context.shape
    owners_n = 2 * ZN
    capacity = slots // owners_n
    half = model // 2
    feats = student_out_weight.shape[1] // 2
    tensor_n = model // (2 * feats)
    z_groups = [[h * ZN + z for z in range(ZN)] for h in range(2)]

    core_swap = [(0, 1), (1, 0)]
    both = ("group", "seq")
    all_pairs = partner_pairs(0) + partner_pairs(owners_n)

    keyval = teacher_keyval[0]
    seg_rows = segment_ids.astype(jnp.bfloat16).reshape(2, HD)
    seg_rows = jnp.concatenate([seg_rows, jnp.zeros((14, HD), jnp.bfloat16)], axis=0)
    passed = lax.ppermute(keyval, "group", [(0, 1)])
    piece = jnp.where(group == 0, keyval[:, :HD], passed[:, HD:])
    piece = jnp.concatenate([piece, seg_rows], axis=0)
    piece, projector = lax.optimization_barrier((piece, projector))
    projector = select_columns(group[None].astype(jnp.int32), projector, tensor_n)
    crossing = lax.dynamic_slice_in_dim(student_out_weight, (1 - group) * feats, feats, axis=1)
    crossing = jnp.concatenate([crossing, jnp.zeros((16, feats), crossing.dtype)], axis=0)
    exchanged = lax.ppermute(jnp.concatenate([crossing, piece], axis=1), both, all_pairs)
    lower = exchanged[:, feats:]
    crossing = exchanged[:256, :feats]
    ring = seq % ZN
    later = (jnp.arange(ZN, dtype=jnp.int32) >= ring) | (high == 0)
    pieces = jnp.where(later[:, None, None], piece[None], lower[None])
    ours = [
        lax.dynamic_slice_in_dim(
            student_context, group * half + side * (half // 2), half // 2, axis=1
        )
        for side in range(2)
    ]
    pieces, query, ours, student_out_weight, owner_table, projector = lax.optimization_barrier(
        (pieces, query, ours, student_out_weight, owner_table, projector)
    )
    mine = lax.all_to_all(
        pieces, "seq", split_axis=0, concat_axis=0, tiled=True, axis_index_groups=z_groups
    )
    below = lax.ppermute(
        lower,
        both,
        [
            (g * 2 * ZN + ZN + z, g * 2 * ZN + ZN + z + 1)
            for g in range(2)
            for z in range(ZN - 1)
        ],
    )
    mine = jnp.concatenate([mine, lower[None], below[None]], axis=0)

    theirs = [lax.ppermute(part, both, all_pairs) for part in ours]

    width = query.shape[1] // 2
    other_query = lax.ppermute(query[:, width:], "group", [(0, 1)])
    query = jnp.where(group == 0, query[:, :width], other_query)
    seg_query = segment_ids.astype(jnp.float32)[:, None]
    info = jnp.stack([seq, group]).astype(jnp.int32)

    weight = lax.dynamic_slice_in_dim(student_out_weight, group * feats, feats, axis=1)
    weight = jnp.where(group == high, weight, crossing)
    weight = jnp.broadcast_to(weight[None], (ZN,) + weight.shape)

    owners_all = owner_table[:, 0]
    owners = lax.dynamic_slice_in_dim(owners_all, seq * tok, tok)
    index = jnp.arange(tok, dtype=jnp.int32)
    ranks = jnp.sum(
        ((owners[:, None] == owners[None, :]) & (index[None, :] < index[:, None])).astype(
            jnp.int32
        ),
        axis=1,
    )
    slot = owners * capacity + ranks
    route = (jnp.arange(slots, dtype=jnp.int32)[:, None] == slot[None, :]).astype(jnp.bfloat16)
    pair_owners = jnp.stack([seq, (seq + ZN) % owners_n])
    counts = jnp.sum(
        (owners_all.reshape(owners_n, tok, 1) == pair_owners[None, None, :]).astype(jnp.int32),
        axis=1,
    )
    live = jnp.arange(capacity, dtype=jnp.int32)[None, :, None] < counts[:, None, :]
    scale = live.reshape(slots, 2, 1).astype(jnp.float32) / tok
    scale = jnp.broadcast_to(scale, (slots, 2, feats // 2)).reshape(slots, feats)
    mine, query, seg_query, info, weight, route, scale, theirs[0] = (
        lax.optimization_barrier(
            (mine, query, seg_query, info, weight, route, scale, theirs[0])
        )
    )
    other = lax.ppermute(mine, "group", core_swap)
    weight = lax.all_to_all(
        weight, "seq", split_axis=0, concat_axis=0, tiled=True, axis_index_groups=z_groups
    ).reshape(half, feats)
    context = attend(info, query, seg_query, mine, other)
    place = info

    other_context = lax.ppermute(context, "group", core_swap)
    context = jnp.where(
        group == 0,
        jnp.concatenate([context, other_context], axis=1),
        jnp.concatenate([other_context, context], axis=1),
    )
    partial = project(context, projector)
    partial, theirs[1] = lax.optimization_barrier((partial, theirs[1]))
    partial = lax.all_to_all(partial, "tensor", split_axis=0, concat_axis=0, tiled=True)
    output, given = on_core(
        student_kernel,
        "student",
        [
            jax.ShapeDtypeStruct((slots, feats), jnp.float32),
            jax.ShapeDtypeStruct((slots, feats), jnp.bfloat16),
        ],
        4 * slots * half * feats,
        place,
        *ours,
        *theirs,
        weight,
    )
    output = output + lax.ppermute(given, "group", core_swap).astype(jnp.float32)
    partial, output = lax.optimization_barrier((partial, output))
    target = jnp.sum(partial.astype(jnp.float32), axis=0).astype(jnp.bfloat16)

    routed = jnp.dot(route, target, preferred_element_type=jnp.float32).astype(jnp.bfloat16)
    routed = routed.reshape(2, ZN, capacity, feats)
    lanes = feats // 2
    routed = jnp.stack(
        [
            jnp.concatenate([routed[0, :, :, :lanes], routed[1, :, :, :lanes]], axis=-1),
            jnp.concatenate([routed[1, :, :, lanes:], routed[0, :, :, lanes:]], axis=-1),
        ]
    ).reshape(owners_n, capacity, feats)
    routed = lax.all_to_all(
        routed, "seq", split_axis=0, concat_axis=0, tiled=True
    ).reshape(slots, feats)
    residual = ((output - routed.astype(jnp.float32)) * scale).astype(jnp.bfloat16)

    gradient = on_core(
        gradient_kernel,
        "gradient",
        jax.ShapeDtypeStruct((ZN, half // ZN, feats), jnp.bfloat16),
        4 * slots * half * feats,
        place,
        *ours,
        *theirs,
        residual,
        lax.ppermute(residual, "group", core_swap),
    )
    gradient = lax.all_to_all(
        gradient,
        "seq",
        split_axis=0,
        concat_axis=0,
        tiled=True,
        axis_index_groups=z_groups,
    )
    gradient = jnp.sum(gradient.astype(jnp.float32), axis=0).astype(jnp.bfloat16)

    straight = lax.ppermute(gradient, both, [(z, 2 * ZN + z) for z in range(ZN)])
    crossed = lax.ppermute(
        gradient,
        both,
        [(ZN + z, 2 * ZN + z) for z in range(ZN)] + [(2 * ZN + z, 3 * ZN + z) for z in range(ZN)],
    )
    whole = jnp.where(
        high == 0,
        jnp.concatenate([straight, crossed], axis=1),
        jnp.concatenate([crossed, gradient], axis=1),
    )
    return jnp.where(group == 1, whole.astype(jnp.float32), 0.0)[None]


def solution(mesh):
    placed = (
        P("group", "seq", "tensor"),
        P("group", "seq", "tensor"),
        P("seq"),
        P("tensor", None),
        P(),
        P("seq", None),
        P("seq", "tensor"),
    )
    return jax.shard_map(
        shards, mesh=mesh, in_specs=placed, out_specs=P("group", "seq", "tensor"), check_vma=False
    )
```

```python
import functools

import jax
import jax.numpy as jnp
from jax import lax
from jax.experimental import pallas as pl
from jax.experimental.pallas import tpu as pltpu
from jax.sharding import PartitionSpec as P

HD = 128
ZN = 8
WINDOW = 9
PIECE = 272
LOW = -1e30


def partner_pairs(base):
    return [(base + i, base + (i + ZN) % (2 * ZN)) for i in range(2 * ZN)]


def attention_kernel(
    info, query, seg_query, mine, other, out, kept, seg_kept, stacked, scores, acc, top
):
    shard = info[0]
    core = info[1]
    tok = query.shape[0]
    heads = query.shape[1] // HD
    scale = (HD**-0.5) * 1.4426950408889634
    seg_q = seg_query[...]
    first_seg = seg_q[0:1, :][0, 0]

    upper = shard // ZN
    ring = lax.rem(shard, ZN)

    def keep_block(step, count):
        place = lax.rem(ring + 1 + step, ZN)
        place = jnp.where(step < ZN, place, step)
        block = jnp.where(place <= ring, upper * ZN + place, place)
        block = jnp.where(place == ZN, ring, block)
        block = jnp.where(place == ZN + 1, ring - 1, block)
        tail = mine[place, 256:272, :].astype(jnp.float32)
        last_seg = tail[1:2, HD - 1 : HD][0, 0]
        wanted = (block >= 0) & (block >= shard - WINDOW) & (block <= shard)
        wanted = wanted & (last_seg >= first_seg) & ((step < ZN) | (upper == 1))

        @pl.when(wanted)
        def _():
            first = mine[place, 0:256, :]
            second = other[place, 0:256, :]
            rows = pl.ds(pl.multiple_of(count * 256, 256), 256)
            kept[rows, 0:HD] = jnp.where(core == 0, first, second)
            kept[rows, HD : 2 * HD] = jnp.where(core == 0, second, first)
            seg_kept[count] = jnp.concatenate([tail[0:1, :], tail[1:2, :]], axis=1)

        return count + wanted.astype(jnp.int32)

    count = lax.fori_loop(ZN, ZN + 2, keep_block, jnp.int32(0))
    count = lax.fori_loop(0, ZN, keep_block, count)

    @pl.when(lax.rem(count, 2) == 1)
    def _():
        kept[pl.ds(pl.multiple_of(count * 256, 256), 256), :] = jnp.zeros(
            (256, 2 * HD), jnp.bfloat16
        )
        seg_kept[count] = jnp.full((1, 256), -1.0, jnp.float32)

    for head in range(heads):
        stacked[head * tok : (head + 1) * tok, :] = query[:, head * HD : (head + 1) * HD]
    top[...] = jnp.full_like(top, LOW)
    acc[...] = jnp.zeros_like(acc)
    causal = lax.broadcasted_iota(jnp.int32, (tok, 256), 1) <= lax.broadcasted_iota(
        jnp.int32, (tok, 256), 0
    )

    def score_pair(pair, carry):
        keys = kept[pl.ds(pl.multiple_of(pair * 512, 512), 512), 0:HD]
        found = lax.dot_general(
            stacked[...], keys, (((1,), (1,)), ((), ())), preferred_element_type=jnp.float32
        )
        for side in range(2):
            index = 2 * pair + side
            allowed = (seg_kept[index] == seg_q) & (causal | (index != count - 1))
            for head in range(heads):
                rows = slice(head * tok, (head + 1) * tok)
                part = jnp.where(allowed, found[rows, side * 256 : (side + 1) * 256], LOW)
                scores[index, rows, :] = part
                top[rows, :] = jnp.maximum(top[rows, :], jnp.maximum(part[:, :HD], part[:, HD:]))
        return carry

    pairs = (count + 1) // 2
    lax.fori_loop(0, pairs, score_pair, 0)
    top[...] = jnp.broadcast_to(jnp.max(top[...], axis=1, keepdims=True), top.shape)

    def mix_pair(pair, carry):
        values = kept[pl.ds(pl.multiple_of(pair * 512, 512), 512), HD : 2 * HD]
        values = jnp.concatenate([values, jnp.ones_like(values)], axis=1)
        best = jnp.concatenate([top[...], top[...]], axis=1)
        weights = jnp.concatenate(
            [
                jnp.exp2((scores[2 * pair + side] - best) * scale).astype(jnp.bfloat16)
                for side in range(2)
            ],
            axis=1,
        )
        acc[...] += jnp.dot(weights, values, preferred_element_type=jnp.float32)
        return carry

    lax.fori_loop(0, pairs, mix_pair, 0)
    for head in range(heads):
        mixed = acc[head * tok : (head + 1) * tok, :]
        out[:, head * HD : (head + 1) * HD] = (mixed[:, :HD] / mixed[:, HD:]).astype(jnp.bfloat16)


def attend(info, query, seg_query, mine, other):
    tok, width = query.shape
    heads = width // HD
    blocks = WINDOW + 1
    vmem = pl.BlockSpec(memory_space=pltpu.VMEM)
    return pl.pallas_call(
        attention_kernel,
        out_shape=jax.ShapeDtypeStruct((tok, width), jnp.bfloat16),
        in_specs=[pl.BlockSpec(memory_space=pltpu.SMEM)] + [pl.BlockSpec()] * 4,
        out_specs=vmem,
        scratch_shapes=[
            pltpu.VMEM((blocks * 256, 2 * HD), jnp.bfloat16),
            pltpu.VMEM((blocks, 1, 256), jnp.float32),
            pltpu.VMEM((heads * tok, HD), jnp.bfloat16),
            pltpu.VMEM((blocks, heads * tok, 256), jnp.float32),
            pltpu.VMEM((heads * tok, 2 * HD), jnp.float32),
            pltpu.VMEM((heads * tok, HD), jnp.float32),
        ],
        compiler_params=pltpu.CompilerParams(vmem_limit_bytes=24 * 1024 * 1024),
        cost_estimate=pl.CostEstimate(
            flops=8 * tok * width * 2560,
            bytes_accessed=4 << 20,
            transcendentals=tok * heads * 2560,
        ),
        name="attend",
    )(info, query, seg_query, mine, other)


def project_kernel(core, context, low, high, out):
    weight = jnp.concatenate([low[...], high[...]], axis=1)
    out[0] = jnp.dot(context[...], weight, preferred_element_type=jnp.float32).astype(jnp.bfloat16)


def project(core, context, projector, tensor_n):
    tok, width = context.shape
    feats = projector.shape[1] // (4 * tensor_n)
    return pl.pallas_call(
        project_kernel,
        out_shape=jax.ShapeDtypeStruct((tensor_n, tok, 2 * feats), jnp.bfloat16),
        grid_spec=pltpu.PrefetchScalarGridSpec(
            num_scalar_prefetch=1,
            grid=(tensor_n,),
            in_specs=[
                pl.BlockSpec((tok, width), lambda i, core: (0, 0)),
                pl.BlockSpec((width, feats), lambda i, core: (0, 4 * i + core[0])),
                pl.BlockSpec((width, feats), lambda i, core: (0, 4 * i + 2 + core[0])),
            ],
            out_specs=pl.BlockSpec((1, tok, 2 * feats), lambda i, core: (i, 0, 0)),
        ),
        compiler_params=pltpu.CompilerParams(vmem_limit_bytes=16 * 1024 * 1024),
        cost_estimate=pl.CostEstimate(
            flops=4 * tok * width * feats * tensor_n,
            bytes_accessed=4 * width * feats * tensor_n,
            transcendentals=0,
        ),
        name="project",
    )(core, context, projector, projector)


def student_kernel(place, ours_low, ours_high, theirs_low, theirs_high, weight, kept, sent):
    core = place[1]
    middle = ours_low.shape[1]

    def product(low, high):
        return jnp.dot(
            low[...], weight[:middle, :], preferred_element_type=jnp.float32
        ) + jnp.dot(high[...], weight[middle:, :], preferred_element_type=jnp.float32)

    own = product(ours_low, ours_high)
    partner = product(theirs_low, theirs_high)
    lanes = own.shape[1] // 2
    first = jnp.concatenate([own[:, :lanes], partner[:, :lanes]], axis=1)
    second = jnp.concatenate([own[:, lanes:], partner[:, lanes:]], axis=1)
    kept[...] = jnp.where(core == 0, first, second)
    sent[...] = jnp.where(core == 0, second, first).astype(jnp.bfloat16)


def gradient_kernel(place, ours_low, ours_high, theirs_low, theirs_high, mine, other, out):
    core = place[1]
    lanes = mine.shape[1] // 2
    first = jnp.where(core == 0, mine[...], other[...])
    second = jnp.where(core == 0, other[...], mine[...])
    own = jnp.concatenate([first[:, :lanes], second[:, :lanes]], axis=1)
    partner = jnp.concatenate([first[:, lanes:], second[:, lanes:]], axis=1)
    over_rows = (((0,), (0,)), ((), ()))
    count, width = out.shape[0] // 2, out.shape[1]
    for side, (ours, theirs) in enumerate(((ours_low, theirs_low), (ours_high, theirs_high))):
        for index in range(count):
            columns = slice(index * width, (index + 1) * width)
            out[side * count + index] = (
                lax.dot_general(ours[:, columns], own, over_rows, preferred_element_type=jnp.float32)
                + lax.dot_general(
                    theirs[:, columns], partner, over_rows, preferred_element_type=jnp.float32
                )
            ).astype(jnp.bfloat16)


def on_core(kernel, name, out_shape, flops, place, *args):
    vmem = pl.BlockSpec(memory_space=pltpu.VMEM)
    return pl.pallas_call(
        kernel,
        out_shape=out_shape,
        in_specs=[pl.BlockSpec(memory_space=pltpu.SMEM)] + [vmem] * len(args),
        out_specs=jax.tree.map(lambda _: vmem, out_shape),
        compiler_params=pltpu.CompilerParams(vmem_limit_bytes=32 * 1024 * 1024),
        cost_estimate=pl.CostEstimate(flops=flops, bytes_accessed=6 << 20, transcendentals=0),
        name=name,
    )(place, *args)


def shards(
    teacher_query,
    teacher_keyval,
    segment_ids,
    projector,
    owner_table,
    student_context,
    student_out_weight,
):
    group = lax.axis_index("group")
    seq = lax.axis_index("seq")
    high = seq // ZN
    query = teacher_query[0]
    tok = query.shape[0]
    slots, model = student_context.shape
    owners_n = 2 * ZN
    capacity = slots // owners_n
    half = model // 2
    feats = student_out_weight.shape[1] // 2
    tensor_n = model // (2 * feats)
    z_groups = [[h * ZN + z for z in range(ZN)] for h in range(2)]

    core_swap = [(0, 1), (1, 0)]
    both = ("group", "seq")
    all_pairs = partner_pairs(0) + partner_pairs(owners_n)

    keyval = teacher_keyval[0]
    seg_rows = segment_ids.astype(jnp.bfloat16).reshape(2, HD)
    seg_rows = jnp.concatenate([seg_rows, jnp.zeros((14, HD), jnp.bfloat16)], axis=0)
    passed = lax.ppermute(keyval, "group", [(0, 1)])
    piece = jnp.where(group == 0, keyval[:, :HD], passed[:, HD:])
    piece = jnp.concatenate([piece, seg_rows], axis=0)
    crossing = lax.dynamic_slice_in_dim(student_out_weight, (1 - group) * feats, feats, axis=1)
    crossing = jnp.concatenate([crossing, jnp.zeros((16, feats), crossing.dtype)], axis=0)
    exchanged = lax.ppermute(jnp.concatenate([crossing, piece], axis=1), both, all_pairs)
    lower = exchanged[:, feats:]
    crossing = exchanged[:256, :feats]
    ring = seq % ZN
    later = (jnp.arange(ZN, dtype=jnp.int32) >= ring) | (high == 0)
    pieces = jnp.where(later[:, None, None], piece[None], lower[None])
    ours = [
        lax.dynamic_slice_in_dim(
            student_context, group * half + side * (half // 2), half // 2, axis=1
        )
        for side in range(2)
    ]
    pieces, query, ours, student_out_weight, owner_table = lax.optimization_barrier(
        (pieces, query, ours, student_out_weight, owner_table)
    )
    mine = lax.all_to_all(
        pieces, "seq", split_axis=0, concat_axis=0, tiled=True, axis_index_groups=z_groups
    )

    theirs = [lax.ppermute(part, both, all_pairs) for part in ours]

    width = query.shape[1] // 2
    other_query = lax.ppermute(query[:, width:], "group", [(0, 1)])
    other_query, lower = lax.optimization_barrier((other_query, lower))
    below = lax.ppermute(
        lower,
        both,
        [
            (g * 2 * ZN + ZN + z, g * 2 * ZN + ZN + z + 1)
            for g in range(2)
            for z in range(ZN - 1)
        ],
    )
    mine = jnp.concatenate([mine, lower[None], below[None]], axis=0)
    query = jnp.where(group == 0, query[:, :width], other_query)
    seg_query = segment_ids.astype(jnp.float32)[:, None]
    info = jnp.stack([seq, group]).astype(jnp.int32)

    weight = lax.dynamic_slice_in_dim(student_out_weight, group * feats, feats, axis=1)
    weight = jnp.where(group == high, weight, crossing)
    weight = jnp.broadcast_to(weight[None], (ZN,) + weight.shape)

    owners_all = owner_table[:, 0]
    owners = lax.dynamic_slice_in_dim(owners_all, seq * tok, tok)
    index = jnp.arange(tok, dtype=jnp.int32)
    ranks = jnp.sum(
        ((owners[:, None] == owners[None, :]) & (index[None, :] < index[:, None])).astype(
            jnp.int32
        ),
        axis=1,
    )
    slot = owners * capacity + ranks
    route = (jnp.arange(slots, dtype=jnp.int32)[:, None] == slot[None, :]).astype(jnp.bfloat16)
    pair_owners = jnp.stack([seq, (seq + ZN) % owners_n])
    counts = jnp.sum(
        (owners_all.reshape(owners_n, tok, 1) == pair_owners[None, None, :]).astype(jnp.int32),
        axis=1,
    )
    live = jnp.arange(capacity, dtype=jnp.int32)[None, :, None] < counts[:, None, :]
    scale = live.reshape(slots, 2, 1).astype(jnp.float32) / tok
    scale = jnp.broadcast_to(scale, (slots, 2, feats // 2)).reshape(slots, feats)
    mine, query, seg_query, info, weight, route, scale, theirs[0] = (
        lax.optimization_barrier(
            (mine, query, seg_query, info, weight, route, scale, theirs[0])
        )
    )
    other = lax.ppermute(mine, "group", core_swap)
    weight = lax.all_to_all(
        weight, "seq", split_axis=0, concat_axis=0, tiled=True, axis_index_groups=z_groups
    ).reshape(half, feats)
    context = attend(info, query, seg_query, mine, other)
    place = info

    other_context = lax.ppermute(context, "group", core_swap)
    context = jnp.where(
        group == 0,
        jnp.concatenate([context, other_context], axis=1),
        jnp.concatenate([other_context, context], axis=1),
    )
    partial = project(group[None].astype(jnp.int32), context, projector, tensor_n)
    partial, theirs[1] = lax.optimization_barrier((partial, theirs[1]))
    partial = lax.all_to_all(partial, "tensor", split_axis=0, concat_axis=0, tiled=True)
    output, given = on_core(
        student_kernel,
        "student",
        [
            jax.ShapeDtypeStruct((slots, feats), jnp.float32),
            jax.ShapeDtypeStruct((slots, feats), jnp.bfloat16),
        ],
        4 * slots * half * feats,
        place,
        *ours,
        *theirs,
        weight,
    )
    output = output + lax.ppermute(given, "group", core_swap).astype(jnp.float32)
    partial, output = lax.optimization_barrier((partial, output))
    target = jnp.sum(partial.astype(jnp.float32), axis=0).astype(jnp.bfloat16)

    routed = jnp.dot(route, target, preferred_element_type=jnp.float32).astype(jnp.bfloat16)
    routed = routed.reshape(2, ZN, capacity, feats)
    lanes = feats // 2
    routed = jnp.stack(
        [
            jnp.concatenate([routed[0, :, :, :lanes], routed[1, :, :, :lanes]], axis=-1),
            jnp.concatenate([routed[1, :, :, lanes:], routed[0, :, :, lanes:]], axis=-1),
        ]
    ).reshape(owners_n, capacity, feats)
    routed = lax.all_to_all(
        routed, "seq", split_axis=0, concat_axis=0, tiled=True
    ).reshape(slots, feats)
    residual = ((output - routed.astype(jnp.float32)) * scale).astype(jnp.bfloat16)

    gradient = on_core(
        gradient_kernel,
        "gradient",
        jax.ShapeDtypeStruct((ZN, half // ZN, feats), jnp.bfloat16),
        4 * slots * half * feats,
        place,
        *ours,
        *theirs,
        residual,
        lax.ppermute(residual, "group", core_swap),
    )
    gradient = lax.all_to_all(
        gradient,
        "seq",
        split_axis=0,
        concat_axis=0,
        tiled=True,
        axis_index_groups=z_groups,
    )
    gradient = jnp.sum(gradient.astype(jnp.float32), axis=0).astype(jnp.bfloat16)

    straight = lax.ppermute(gradient, both, [(z, 2 * ZN + z) for z in range(ZN)])
    crossed = lax.ppermute(
        gradient,
        both,
        [(ZN + z, 2 * ZN + z) for z in range(ZN)] + [(2 * ZN + z, 3 * ZN + z) for z in range(ZN)],
    )
    whole = jnp.where(
        high == 0,
        jnp.concatenate([straight, crossed], axis=1),
        jnp.concatenate([crossed, gradient], axis=1),
    )
    return jnp.where(group == 1, whole.astype(jnp.float32), 0.0)[None]


def solution(mesh):
    placed = (
        P("group", "seq", "tensor"),
        P("group", "seq", "tensor"),
        P("seq"),
        P("tensor", None),
        P(),
        P("seq", None),
        P("seq", "tensor"),
    )
    return jax.shard_map(
        shards, mesh=mesh, in_specs=placed, out_specs=P("group", "seq", "tensor"), check_vma=False
    )
```

```python
import functools

import jax
import jax.numpy as jnp
from jax import lax
from jax.experimental import pallas as pl
from jax.experimental.pallas import tpu as pltpu
from jax.sharding import PartitionSpec as P

HD = 128
ZN = 8
WINDOW = 9
PIECE = 272
LOW = -1e30


def partner_pairs(base):
    return [(base + i, base + (i + ZN) % (2 * ZN)) for i in range(2 * ZN)]


def attention_kernel(
    info, query, seg_query, mine, other, out, kept, seg_kept, stacked, scores, acc, top
):
    shard = info[0]
    core = info[1]
    tok = query.shape[0]
    heads = query.shape[1] // HD
    scale = (HD**-0.5) * 1.4426950408889634
    seg_q = seg_query[...]
    first_seg = seg_q[0:1, :][0, 0]

    upper = shard // ZN
    ring = lax.rem(shard, ZN)

    def keep_block(step, count):
        place = lax.rem(ring + 1 + step, ZN)
        place = jnp.where(step < ZN, place, step)
        block = jnp.where(place <= ring, upper * ZN + place, place)
        block = jnp.where(place == ZN, ring, block)
        block = jnp.where(place == ZN + 1, ring - 1, block)
        tail = mine[place, 256:272, :].astype(jnp.float32)
        last_seg = tail[1:2, HD - 1 : HD][0, 0]
        wanted = (block >= 0) & (block >= shard - WINDOW) & (block <= shard)
        wanted = wanted & (last_seg >= first_seg) & ((step < ZN) | (upper == 1))

        @pl.when(wanted)
        def _():
            first = mine[place, 0:256, :]
            second = other[place, 0:256, :]
            rows = pl.ds(pl.multiple_of(count * 256, 256), 256)
            kept[rows, 0:HD] = jnp.where(core == 0, first, second)
            kept[rows, HD : 2 * HD] = jnp.where(core == 0, second, first)
            seg_kept[count] = jnp.concatenate([tail[0:1, :], tail[1:2, :]], axis=1)

        return count + wanted.astype(jnp.int32)

    count = lax.fori_loop(ZN, ZN + 2, keep_block, jnp.int32(0))
    count = lax.fori_loop(0, ZN, keep_block, count)

    @pl.when(lax.rem(count, 2) == 1)
    def _():
        kept[pl.ds(pl.multiple_of(count * 256, 256), 256), :] = jnp.zeros(
            (256, 2 * HD), jnp.bfloat16
        )
        seg_kept[count] = jnp.full((1, 256), -1.0, jnp.float32)

    for head in range(heads):
        stacked[head * tok : (head + 1) * tok, :] = query[:, head * HD : (head + 1) * HD]
    top[...] = jnp.full_like(top, LOW)
    acc[...] = jnp.zeros_like(acc)
    causal = lax.broadcasted_iota(jnp.int32, (tok, 256), 1) <= lax.broadcasted_iota(
        jnp.int32, (tok, 256), 0
    )

    def score_pair(pair, carry):
        keys = kept[pl.ds(pl.multiple_of(pair * 512, 512), 512), 0:HD]
        found = lax.dot_general(
            stacked[...], keys, (((1,), (1,)), ((), ())), preferred_element_type=jnp.float32
        )
        for side in range(2):
            index = 2 * pair + side
            allowed = (seg_kept[index] == seg_q) & (causal | (index != count - 1))
            for head in range(heads):
                rows = slice(head * tok, (head + 1) * tok)
                part = jnp.where(allowed, found[rows, side * 256 : (side + 1) * 256], LOW)
                scores[index, rows, :] = part
                top[rows, :] = jnp.maximum(top[rows, :], jnp.maximum(part[:, :HD], part[:, HD:]))
        return carry

    pairs = (count + 1) // 2
    lax.fori_loop(0, pairs, score_pair, 0)
    top[...] = jnp.broadcast_to(jnp.max(top[...], axis=1, keepdims=True), top.shape)

    def mix_pair(pair, carry):
        values = kept[pl.ds(pl.multiple_of(pair * 512, 512), 512), HD : 2 * HD]
        values = jnp.concatenate([values, jnp.ones_like(values)], axis=1)
        best = jnp.concatenate([top[...], top[...]], axis=1)
        weights = jnp.concatenate(
            [
                jnp.exp2((scores[2 * pair + side] - best) * scale).astype(jnp.bfloat16)
                for side in range(2)
            ],
            axis=1,
        )
        acc[...] += jnp.dot(weights, values, preferred_element_type=jnp.float32)
        return carry

    lax.fori_loop(0, pairs, mix_pair, 0)
    for head in range(heads):
        mixed = acc[head * tok : (head + 1) * tok, :]
        out[:, head * HD : (head + 1) * HD] = (mixed[:, :HD] / mixed[:, HD:]).astype(jnp.bfloat16)


def attend(info, query, seg_query, mine, other):
    tok, width = query.shape
    heads = width // HD
    blocks = WINDOW + 1
    vmem = pl.BlockSpec(memory_space=pltpu.VMEM)
    return pl.pallas_call(
        attention_kernel,
        out_shape=jax.ShapeDtypeStruct((tok, width), jnp.bfloat16),
        in_specs=[pl.BlockSpec(memory_space=pltpu.SMEM)] + [pl.BlockSpec()] * 4,
        out_specs=vmem,
        scratch_shapes=[
            pltpu.VMEM((blocks * 256, 2 * HD), jnp.bfloat16),
            pltpu.VMEM((blocks, 1, 256), jnp.float32),
            pltpu.VMEM((heads * tok, HD), jnp.bfloat16),
            pltpu.VMEM((blocks, heads * tok, 256), jnp.float32),
            pltpu.VMEM((heads * tok, 2 * HD), jnp.float32),
            pltpu.VMEM((heads * tok, HD), jnp.float32),
        ],
        compiler_params=pltpu.CompilerParams(vmem_limit_bytes=24 * 1024 * 1024),
        cost_estimate=pl.CostEstimate(
            flops=8 * tok * width * 2560,
            bytes_accessed=4 << 20,
            transcendentals=tok * heads * 2560,
        ),
        name="attend",
    )(info, query, seg_query, mine, other)


def project_kernel(core, context, low, high, out):
    weight = jnp.concatenate([low[...], high[...]], axis=1)
    out[0] = jnp.dot(context[...], weight, preferred_element_type=jnp.float32).astype(jnp.bfloat16)


def project(core, context, projector, tensor_n):
    tok, width = context.shape
    feats = projector.shape[1] // (4 * tensor_n)
    return pl.pallas_call(
        project_kernel,
        out_shape=jax.ShapeDtypeStruct((tensor_n, tok, 2 * feats), jnp.bfloat16),
        grid_spec=pltpu.PrefetchScalarGridSpec(
            num_scalar_prefetch=1,
            grid=(tensor_n,),
            in_specs=[
                pl.BlockSpec((tok, width), lambda i, core: (0, 0)),
                pl.BlockSpec((width, feats), lambda i, core: (0, 4 * i + core[0])),
                pl.BlockSpec((width, feats), lambda i, core: (0, 4 * i + 2 + core[0])),
            ],
            out_specs=pl.BlockSpec((1, tok, 2 * feats), lambda i, core: (i, 0, 0)),
        ),
        compiler_params=pltpu.CompilerParams(vmem_limit_bytes=16 * 1024 * 1024),
        cost_estimate=pl.CostEstimate(
            flops=4 * tok * width * feats * tensor_n,
            bytes_accessed=4 * width * feats * tensor_n,
            transcendentals=0,
        ),
        name="project",
    )(core, context, projector, projector)


def student_kernel(place, ours_low, ours_high, theirs_low, theirs_high, weight, kept, sent):
    core = place[1]
    middle = ours_low.shape[1]

    def product(low, high):
        return jnp.dot(
            low[...], weight[:middle, :], preferred_element_type=jnp.float32
        ) + jnp.dot(high[...], weight[middle:, :], preferred_element_type=jnp.float32)

    own = product(ours_low, ours_high)
    partner = product(theirs_low, theirs_high)
    lanes = own.shape[1] // 2
    first = jnp.concatenate([own[:, :lanes], partner[:, :lanes]], axis=1)
    second = jnp.concatenate([own[:, lanes:], partner[:, lanes:]], axis=1)
    kept[...] = jnp.where(core == 0, first, second)
    sent[...] = jnp.where(core == 0, second, first).astype(jnp.bfloat16)


def gradient_kernel(place, ours_low, ours_high, theirs_low, theirs_high, mine, other, out):
    core = place[1]
    lanes = mine.shape[1] // 2
    first = jnp.where(core == 0, mine[...], other[...])
    second = jnp.where(core == 0, other[...], mine[...])
    own = jnp.concatenate([first[:, :lanes], second[:, :lanes]], axis=1)
    partner = jnp.concatenate([first[:, lanes:], second[:, lanes:]], axis=1)
    over_rows = (((0,), (0,)), ((), ()))
    count, width = out.shape[0] // 2, out.shape[1]
    for side, (ours, theirs) in enumerate(((ours_low, theirs_low), (ours_high, theirs_high))):
        for index in range(count):
            columns = slice(index * width, (index + 1) * width)
            out[side * count + index] = (
                lax.dot_general(ours[:, columns], own, over_rows, preferred_element_type=jnp.float32)
                + lax.dot_general(
                    theirs[:, columns], partner, over_rows, preferred_element_type=jnp.float32
                )
            ).astype(jnp.bfloat16)


def on_core(kernel, name, out_shape, flops, place, *args):
    vmem = pl.BlockSpec(memory_space=pltpu.VMEM)
    return pl.pallas_call(
        kernel,
        out_shape=out_shape,
        in_specs=[pl.BlockSpec(memory_space=pltpu.SMEM)] + [vmem] * len(args),
        out_specs=jax.tree.map(lambda _: vmem, out_shape),
        compiler_params=pltpu.CompilerParams(vmem_limit_bytes=32 * 1024 * 1024),
        cost_estimate=pl.CostEstimate(flops=flops, bytes_accessed=6 << 20, transcendentals=0),
        name=name,
    )(place, *args)


def shards(
    teacher_query,
    teacher_keyval,
    segment_ids,
    projector,
    owner_table,
    student_context,
    student_out_weight,
):
    group = lax.axis_index("group")
    seq = lax.axis_index("seq")
    high = seq // ZN
    query = teacher_query[0]
    tok = query.shape[0]
    slots, model = student_context.shape
    owners_n = 2 * ZN
    capacity = slots // owners_n
    half = model // 2
    feats = student_out_weight.shape[1] // 2
    tensor_n = model // (2 * feats)
    z_groups = [[h * ZN + z for z in range(ZN)] for h in range(2)]

    core_swap = [(0, 1), (1, 0)]
    both = ("group", "seq")
    all_pairs = partner_pairs(0) + partner_pairs(owners_n)

    keyval = teacher_keyval[0]
    seg_rows = segment_ids.astype(jnp.bfloat16).reshape(2, HD)
    seg_rows = jnp.concatenate([seg_rows, jnp.zeros((14, HD), jnp.bfloat16)], axis=0)
    passed = lax.ppermute(keyval, "group", [(0, 1)])
    piece = jnp.where(group == 0, keyval[:, :HD], passed[:, HD:])
    piece = jnp.concatenate([piece, seg_rows], axis=0)
    column_half = jnp.where(group == 1, high, 1 - high)
    crossing = lax.dynamic_slice_in_dim(student_out_weight, (1 - high) * feats, feats, axis=1)
    crossing = jnp.concatenate([crossing, jnp.zeros((16, feats), crossing.dtype)], axis=0)
    exchanged = lax.ppermute(jnp.concatenate([crossing, piece], axis=1), both, all_pairs)
    lower = exchanged[:, feats:]
    crossing = exchanged[:256, :feats]
    ring = seq % ZN
    later = (jnp.arange(ZN, dtype=jnp.int32) >= ring) | (high == 0)
    pieces = jnp.where(later[:, None, None], piece[None], lower[None])
    def column_parts(rows, place):
        return [
            lax.dynamic_slice_in_dim(rows, place * half + side * (half // 2), half // 2, axis=1)
            for side in range(2)
        ]

    sent = column_parts(student_context, 1 - column_half)
    pieces, query, sent, student_context, student_out_weight, owner_table = (
        lax.optimization_barrier(
            (pieces, query, sent, student_context, student_out_weight, owner_table)
        )
    )
    mine = lax.all_to_all(
        pieces, "seq", split_axis=0, concat_axis=0, tiled=True, axis_index_groups=z_groups
    )

    theirs = [lax.ppermute(part, both, all_pairs) for part in sent]

    width = query.shape[1] // 2
    other_query = lax.ppermute(query[:, width:], "group", [(0, 1)])
    weight = lax.dynamic_slice_in_dim(student_out_weight, high * feats, feats, axis=1)
    weight = jnp.where(group == 1, weight, crossing)
    weight = jnp.broadcast_to(weight[None], (ZN,) + weight.shape)
    other_query, lower, weight = lax.optimization_barrier((other_query, lower, weight))
    below = lax.ppermute(
        lower,
        both,
        [
            (g * 2 * ZN + ZN + z, g * 2 * ZN + ZN + z + 1)
            for g in range(2)
            for z in range(ZN - 1)
        ],
    )
    query = jnp.where(group == 0, query[:, :width], other_query)
    seg_query = segment_ids.astype(jnp.float32)[:, None]
    info = jnp.stack([seq, group]).astype(jnp.int32)

    owners_all = owner_table[:, 0]
    owners = lax.dynamic_slice_in_dim(owners_all, seq * tok, tok)
    index = jnp.arange(tok, dtype=jnp.int32)
    ranks = jnp.sum(
        ((owners[:, None] == owners[None, :]) & (index[None, :] < index[:, None])).astype(
            jnp.int32
        ),
        axis=1,
    )
    slot = owners * capacity + ranks
    route = (jnp.arange(slots, dtype=jnp.int32)[:, None] == slot[None, :]).astype(jnp.bfloat16)
    pair_owners = jnp.stack([seq, (seq + ZN) % owners_n])
    counts = jnp.sum(
        (owners_all.reshape(owners_n, tok, 1) == pair_owners[None, None, :]).astype(jnp.int32),
        axis=1,
    )
    live = jnp.arange(capacity, dtype=jnp.int32)[None, :, None] < counts[:, None, :]
    scale = live.reshape(slots, 2, 1).astype(jnp.float32) / tok
    scale = jnp.broadcast_to(scale, (slots, 2, feats // 2)).reshape(slots, feats)
    mine, weight, below, query, seg_query, info, route, scale = lax.optimization_barrier(
        (mine, weight, below, query, seg_query, info, route, scale)
    )
    weight = lax.all_to_all(
        weight, "seq", split_axis=0, concat_axis=0, tiled=True, axis_index_groups=z_groups
    ).reshape(half, feats)
    mine = jnp.concatenate([mine, lower[None], below[None]], axis=0)
    mine, theirs[0] = lax.optimization_barrier((mine, theirs[0]))
    other = lax.ppermute(mine, "group", core_swap)
    context = attend(info, query, seg_query, mine, other)
    place = info
    ours = column_parts(student_context, column_half)

    other_context = lax.ppermute(context, "group", core_swap)
    context = jnp.where(
        group == 0,
        jnp.concatenate([context, other_context], axis=1),
        jnp.concatenate([other_context, context], axis=1),
    )
    partial = project(group[None].astype(jnp.int32), context, projector, tensor_n)
    partial, theirs[1] = lax.optimization_barrier((partial, theirs[1]))
    partial = lax.all_to_all(partial, "tensor", split_axis=0, concat_axis=0, tiled=True)
    output, given = on_core(
        student_kernel,
        "student",
        [
            jax.ShapeDtypeStruct((slots, feats), jnp.float32),
            jax.ShapeDtypeStruct((slots, feats), jnp.bfloat16),
        ],
        4 * slots * half * feats,
        place,
        *ours,
        *theirs,
        weight,
    )
    output = output + lax.ppermute(given, "group", core_swap).astype(jnp.float32)
    partial, output = lax.optimization_barrier((partial, output))
    target = jnp.sum(partial.astype(jnp.float32), axis=0).astype(jnp.bfloat16)

    routed = jnp.dot(route, target, preferred_element_type=jnp.float32).astype(jnp.bfloat16)
    routed = routed.reshape(2, ZN, capacity, feats)
    lanes = feats // 2
    routed = jnp.stack(
        [
            jnp.concatenate([routed[0, :, :, :lanes], routed[1, :, :, :lanes]], axis=-1),
            jnp.concatenate([routed[1, :, :, lanes:], routed[0, :, :, lanes:]], axis=-1),
        ]
    ).reshape(owners_n, capacity, feats)
    routed = lax.all_to_all(
        routed, "seq", split_axis=0, concat_axis=0, tiled=True
    ).reshape(slots, feats)
    residual = ((output - routed.astype(jnp.float32)) * scale).astype(jnp.bfloat16)

    gradient = on_core(
        gradient_kernel,
        "gradient",
        jax.ShapeDtypeStruct((ZN, half // ZN, feats), jnp.bfloat16),
        4 * slots * half * feats,
        place,
        *ours,
        *theirs,
        residual,
        lax.ppermute(residual, "group", core_swap),
    )
    gradient = lax.all_to_all(
        gradient,
        "seq",
        split_axis=0,
        concat_axis=0,
        tiled=True,
        axis_index_groups=z_groups,
    )
    gradient = jnp.sum(gradient.astype(jnp.float32), axis=0).astype(jnp.bfloat16)

    passed = lax.ppermute(
        gradient,
        both,
        [(h * ZN + z, (3 - h) * ZN + z) for h in range(2) for z in range(ZN)],
    )
    whole = jnp.where(
        high == 0,
        jnp.concatenate([gradient, passed], axis=1),
        jnp.concatenate([passed, gradient], axis=1),
    )
    return jnp.where(group == 1, whole.astype(jnp.float32), 0.0)[None]


def solution(mesh):
    placed = (
        P("group", "seq", "tensor"),
        P("group", "seq", "tensor"),
        P("seq"),
        P("tensor", None),
        P(),
        P("seq", None),
        P("seq", "tensor"),
    )
    return jax.shard_map(
        shards, mesh=mesh, in_specs=placed, out_specs=P("group", "seq", "tensor"), check_vma=False
    )
```

```python
import functools

import jax
import jax.numpy as jnp
from jax import lax
from jax.experimental import pallas as pl
from jax.experimental.pallas import tpu as pltpu
from jax.sharding import PartitionSpec as P

HD = 128
ZN = 8
WINDOW = 9
PIECE = 272
LOW = -1e30


def partner_pairs(base):
    return [(base + i, base + (i + ZN) % (2 * ZN)) for i in range(2 * ZN)]


def attention_kernel(
    info, query, seg_query, mine, other, out, kept, seg_kept, stacked, scores, acc, top
):
    shard = info[0]
    core = info[1]
    tok = query.shape[0]
    heads = query.shape[1] // HD
    scale = (HD**-0.5) * 1.4426950408889634
    seg_q = seg_query[...]
    first_seg = seg_q[0:1, :][0, 0]

    upper = shard // ZN
    ring = lax.rem(shard, ZN)

    def keep_block(step, count):
        place = lax.rem(ring + 1 + step, ZN)
        place = jnp.where(step < ZN, place, step)
        block = jnp.where(place <= ring, upper * ZN + place, place)
        block = jnp.where(place == ZN, ring, block)
        block = jnp.where(place == ZN + 1, ring - 1, block)
        tail = mine[place, 256:272, :].astype(jnp.float32)
        last_seg = tail[1:2, HD - 1 : HD][0, 0]
        wanted = (block >= 0) & (block >= shard - WINDOW) & (block <= shard)
        wanted = wanted & (last_seg >= first_seg) & ((step < ZN) | (upper == 1))

        @pl.when(wanted)
        def _():
            first = mine[place, 0:256, :]
            second = other[place, 0:256, :]
            rows = pl.ds(pl.multiple_of(count * 256, 256), 256)
            kept[rows, 0:HD] = jnp.where(core == 0, first, second)
            kept[rows, HD : 2 * HD] = jnp.where(core == 0, second, first)
            seg_kept[count] = jnp.concatenate([tail[0:1, :], tail[1:2, :]], axis=1)

        return count + wanted.astype(jnp.int32)

    count = lax.fori_loop(ZN, ZN + 2, keep_block, jnp.int32(0))
    count = lax.fori_loop(0, ZN, keep_block, count)

    @pl.when(lax.rem(count, 2) == 1)
    def _():
        kept[pl.ds(pl.multiple_of(count * 256, 256), 256), :] = jnp.zeros(
            (256, 2 * HD), jnp.bfloat16
        )
        seg_kept[count] = jnp.full((1, 256), -1.0, jnp.float32)

    for head in range(heads):
        stacked[head * tok : (head + 1) * tok, :] = query[:, head * HD : (head + 1) * HD]
    top[...] = jnp.full_like(top, LOW)
    acc[...] = jnp.zeros_like(acc)
    causal = lax.broadcasted_iota(jnp.int32, (tok, 256), 1) <= lax.broadcasted_iota(
        jnp.int32, (tok, 256), 0
    )

    def score_pair(pair, carry):
        keys = kept[pl.ds(pl.multiple_of(pair * 512, 512), 512), 0:HD]
        found = lax.dot_general(
            stacked[...], keys, (((1,), (1,)), ((), ())), preferred_element_type=jnp.float32
        )
        for side in range(2):
            index = 2 * pair + side
            allowed = (seg_kept[index] == seg_q) & (causal | (index != count - 1))
            for head in range(heads):
                rows = slice(head * tok, (head + 1) * tok)
                part = jnp.where(allowed, found[rows, side * 256 : (side + 1) * 256], LOW)
                scores[index, rows, :] = part
                top[rows, :] = jnp.maximum(top[rows, :], jnp.maximum(part[:, :HD], part[:, HD:]))
        return carry

    pairs = (count + 1) // 2
    lax.fori_loop(0, pairs, score_pair, 0)
    top[...] = jnp.broadcast_to(jnp.max(top[...], axis=1, keepdims=True), top.shape)

    def mix_pair(pair, carry):
        values = kept[pl.ds(pl.multiple_of(pair * 512, 512), 512), HD : 2 * HD]
        values = jnp.concatenate([values, jnp.ones_like(values)], axis=1)
        best = jnp.concatenate([top[...], top[...]], axis=1)
        weights = jnp.concatenate(
            [
                jnp.exp2((scores[2 * pair + side] - best) * scale).astype(jnp.bfloat16)
                for side in range(2)
            ],
            axis=1,
        )
        acc[...] += jnp.dot(weights, values, preferred_element_type=jnp.float32)
        return carry

    lax.fori_loop(0, pairs, mix_pair, 0)
    for head in range(heads):
        mixed = acc[head * tok : (head + 1) * tok, :]
        out[:, head * HD : (head + 1) * HD] = (mixed[:, :HD] / mixed[:, HD:]).astype(jnp.bfloat16)


def attend(info, query, seg_query, mine, other):
    tok, width = query.shape
    heads = width // HD
    blocks = WINDOW + 1
    vmem = pl.BlockSpec(memory_space=pltpu.VMEM)
    return pl.pallas_call(
        attention_kernel,
        out_shape=jax.ShapeDtypeStruct((tok, width), jnp.bfloat16),
        in_specs=[pl.BlockSpec(memory_space=pltpu.SMEM)] + [pl.BlockSpec()] * 4,
        out_specs=vmem,
        scratch_shapes=[
            pltpu.VMEM((blocks * 256, 2 * HD), jnp.bfloat16),
            pltpu.VMEM((blocks, 1, 256), jnp.float32),
            pltpu.VMEM((heads * tok, HD), jnp.bfloat16),
            pltpu.VMEM((blocks, heads * tok, 256), jnp.float32),
            pltpu.VMEM((heads * tok, 2 * HD), jnp.float32),
            pltpu.VMEM((heads * tok, HD), jnp.float32),
        ],
        compiler_params=pltpu.CompilerParams(vmem_limit_bytes=24 * 1024 * 1024),
        cost_estimate=pl.CostEstimate(
            flops=8 * tok * width * 2560,
            bytes_accessed=4 << 20,
            transcendentals=tok * heads * 2560,
        ),
        name="attend",
    )(info, query, seg_query, mine, other)


def project_kernel(core, context, low, high, out):
    weight = jnp.concatenate([low[...], high[...]], axis=1)
    out[0] = jnp.dot(context[...], weight, preferred_element_type=jnp.float32).astype(jnp.bfloat16)


def project(core, context, projector, tensor_n):
    tok, width = context.shape
    feats = projector.shape[1] // (4 * tensor_n)
    return pl.pallas_call(
        project_kernel,
        out_shape=jax.ShapeDtypeStruct((tensor_n, tok, 2 * feats), jnp.bfloat16),
        grid_spec=pltpu.PrefetchScalarGridSpec(
            num_scalar_prefetch=1,
            grid=(tensor_n,),
            in_specs=[
                pl.BlockSpec((tok, width), lambda i, core: (0, 0)),
                pl.BlockSpec((width, feats), lambda i, core: (0, 4 * i + core[0])),
                pl.BlockSpec((width, feats), lambda i, core: (0, 4 * i + 2 + core[0])),
            ],
            out_specs=pl.BlockSpec((1, tok, 2 * feats), lambda i, core: (i, 0, 0)),
        ),
        compiler_params=pltpu.CompilerParams(vmem_limit_bytes=16 * 1024 * 1024),
        cost_estimate=pl.CostEstimate(
            flops=4 * tok * width * feats * tensor_n,
            bytes_accessed=4 * width * feats * tensor_n,
            transcendentals=0,
        ),
        name="project",
    )(core, context, projector, projector)


def route_kernel(route, partial, out):
    target = partial[0].astype(jnp.float32)
    for index in range(1, partial.shape[0]):
        target = target + partial[index].astype(jnp.float32)
    routed = jnp.dot(
        route[...], target.astype(jnp.bfloat16), preferred_element_type=jnp.float32
    ).astype(jnp.bfloat16)
    rows, lanes = out.shape[1], out.shape[2] // 2
    low, high = routed[:rows], routed[rows:]
    out[0] = jnp.concatenate([low[:, :lanes], high[:, :lanes]], axis=1)
    out[1] = jnp.concatenate([high[:, lanes:], low[:, lanes:]], axis=1)


def student_kernel(place, ours_low, ours_high, theirs_low, theirs_high, weight, kept, sent):
    core = place[1]
    middle = ours_low.shape[1]

    def product(low, high):
        return jnp.dot(
            low[...], weight[:middle, :], preferred_element_type=jnp.float32
        ) + jnp.dot(high[...], weight[middle:, :], preferred_element_type=jnp.float32)

    own = product(ours_low, ours_high)
    partner = product(theirs_low, theirs_high)
    lanes = own.shape[1] // 2
    first = jnp.concatenate([own[:, :lanes], partner[:, :lanes]], axis=1)
    second = jnp.concatenate([own[:, lanes:], partner[:, lanes:]], axis=1)
    kept[...] = jnp.where(core == 0, first, second)
    sent[...] = jnp.where(core == 0, second, first).astype(jnp.bfloat16)


def gradient_kernel(place, ours_low, ours_high, theirs_low, theirs_high, mine, other, out):
    core = place[1]
    lanes = mine.shape[1] // 2
    first = jnp.where(core == 0, mine[...], other[...])
    second = jnp.where(core == 0, other[...], mine[...])
    own = jnp.concatenate([first[:, :lanes], second[:, :lanes]], axis=1)
    partner = jnp.concatenate([first[:, lanes:], second[:, lanes:]], axis=1)
    over_rows = (((0,), (0,)), ((), ()))
    count, width = out.shape[0] // 2, out.shape[1]
    for side, (ours, theirs) in enumerate(((ours_low, theirs_low), (ours_high, theirs_high))):
        for index in range(count):
            columns = slice(index * width, (index + 1) * width)
            out[side * count + index] = (
                lax.dot_general(ours[:, columns], own, over_rows, preferred_element_type=jnp.float32)
                + lax.dot_general(
                    theirs[:, columns], partner, over_rows, preferred_element_type=jnp.float32
                )
            ).astype(jnp.bfloat16)


def on_core(kernel, name, out_shape, flops, place, *args):
    vmem = pl.BlockSpec(memory_space=pltpu.VMEM)
    return pl.pallas_call(
        kernel,
        out_shape=out_shape,
        in_specs=[pl.BlockSpec(memory_space=pltpu.SMEM)] + [vmem] * len(args),
        out_specs=jax.tree.map(lambda _: vmem, out_shape),
        compiler_params=pltpu.CompilerParams(vmem_limit_bytes=32 * 1024 * 1024),
        cost_estimate=pl.CostEstimate(flops=flops, bytes_accessed=6 << 20, transcendentals=0),
        name=name,
    )(place, *args)


def shards(
    teacher_query,
    teacher_keyval,
    segment_ids,
    projector,
    owner_table,
    student_context,
    student_out_weight,
):
    group = lax.axis_index("group")
    seq = lax.axis_index("seq")
    high = seq // ZN
    query = teacher_query[0]
    tok = query.shape[0]
    slots, model = student_context.shape
    owners_n = 2 * ZN
    capacity = slots // owners_n
    half = model // 2
    feats = student_out_weight.shape[1] // 2
    tensor_n = model // (2 * feats)
    z_groups = [[h * ZN + z for z in range(ZN)] for h in range(2)]

    core_swap = [(0, 1), (1, 0)]
    both = ("group", "seq")
    all_pairs = partner_pairs(0) + partner_pairs(owners_n)

    keyval = teacher_keyval[0]
    seg_rows = segment_ids.astype(jnp.bfloat16).reshape(2, HD)
    seg_rows = jnp.concatenate([seg_rows, jnp.zeros((14, HD), jnp.bfloat16)], axis=0)
    passed = lax.ppermute(keyval, "group", [(0, 1)])
    piece = jnp.where(group == 0, keyval[:, :HD], passed[:, HD:])
    piece = jnp.concatenate([piece, seg_rows], axis=0)
    column_half = jnp.where(group == 1, high, 1 - high)
    crossing = lax.dynamic_slice_in_dim(student_out_weight, (1 - high) * feats, feats, axis=1)
    crossing = jnp.concatenate([crossing, jnp.zeros((16, feats), crossing.dtype)], axis=0)
    exchanged = lax.ppermute(jnp.concatenate([crossing, piece], axis=1), both, all_pairs)
    lower = exchanged[:, feats:]
    crossing = exchanged[:256, :feats]
    ring = seq % ZN
    later = (jnp.arange(ZN, dtype=jnp.int32) >= ring) | (high == 0)
    pieces = jnp.where(later[:, None, None], piece[None], lower[None])
    def column_parts(rows, place):
        return [
            lax.dynamic_slice_in_dim(rows, place * half + side * (half // 2), half // 2, axis=1)
            for side in range(2)
        ]

    sent = column_parts(student_context, 1 - column_half)
    pieces, query, sent, student_context, student_out_weight, owner_table = (
        lax.optimization_barrier(
            (pieces, query, sent, student_context, student_out_weight, owner_table)
        )
    )
    mine = lax.all_to_all(
        pieces, "seq", split_axis=0, concat_axis=0, tiled=True, axis_index_groups=z_groups
    )

    theirs = [lax.ppermute(part, both, all_pairs) for part in sent]

    width = query.shape[1] // 2
    other_query = lax.ppermute(query[:, width:], "group", [(0, 1)])
    weight = lax.dynamic_slice_in_dim(student_out_weight, high * feats, feats, axis=1)
    weight = jnp.where(group == 1, weight, crossing)
    weight = jnp.broadcast_to(weight[None], (ZN,) + weight.shape)
    other_query, lower, weight = lax.optimization_barrier((other_query, lower, weight))
    below = lax.ppermute(
        lower,
        both,
        [
            (g * 2 * ZN + ZN + z, g * 2 * ZN + ZN + z + 1)
            for g in range(2)
            for z in range(ZN - 1)
        ],
    )
    query = jnp.where(group == 0, query[:, :width], other_query)
    seg_query = segment_ids.astype(jnp.float32)[:, None]
    info = jnp.stack([seq, group]).astype(jnp.int32)

    owners_all = owner_table[:, 0]
    owners = lax.dynamic_slice_in_dim(owners_all, seq * tok, tok)
    index = jnp.arange(tok, dtype=jnp.int32)
    ranks = jnp.sum(
        ((owners[:, None] == owners[None, :]) & (index[None, :] < index[:, None])).astype(
            jnp.int32
        ),
        axis=1,
    )
    slot = owners * capacity + ranks
    route = (jnp.arange(slots, dtype=jnp.int32)[:, None] == slot[None, :]).astype(jnp.bfloat16)
    pair_owners = jnp.stack([seq, (seq + ZN) % owners_n])
    counts = jnp.sum(
        (owners_all.reshape(owners_n, tok, 1) == pair_owners[None, None, :]).astype(jnp.int32),
        axis=1,
    )
    live = jnp.arange(capacity, dtype=jnp.int32)[None, :, None] < counts[:, None, :]
    scale = live.reshape(slots, 2, 1).astype(jnp.float32) / tok
    scale = jnp.broadcast_to(scale, (slots, 2, feats // 2)).reshape(slots, feats)
    mine, weight, below, query, seg_query, info, route, scale = lax.optimization_barrier(
        (mine, weight, below, query, seg_query, info, route, scale)
    )
    weight = lax.all_to_all(
        weight, "seq", split_axis=0, concat_axis=0, tiled=True, axis_index_groups=z_groups
    ).reshape(half, feats)
    mine = jnp.concatenate([mine, lower[None], below[None]], axis=0)
    mine, theirs[0] = lax.optimization_barrier((mine, theirs[0]))
    other = lax.ppermute(mine, "group", core_swap)
    context = attend(info, query, seg_query, mine, other)
    place = info
    ours = column_parts(student_context, column_half)

    other_context = lax.ppermute(context, "group", core_swap)
    context = jnp.where(
        group == 0,
        jnp.concatenate([context, other_context], axis=1),
        jnp.concatenate([other_context, context], axis=1),
    )
    partial = project(group[None].astype(jnp.int32), context, projector, tensor_n)
    partial, theirs[1] = lax.optimization_barrier((partial, theirs[1]))
    partial = lax.all_to_all(partial, "tensor", split_axis=0, concat_axis=0, tiled=True)
    output, given = on_core(
        student_kernel,
        "student",
        [
            jax.ShapeDtypeStruct((slots, feats), jnp.float32),
            jax.ShapeDtypeStruct((slots, feats), jnp.bfloat16),
        ],
        4 * slots * half * feats,
        place,
        *ours,
        *theirs,
        weight,
    )
    output = output + lax.ppermute(given, "group", core_swap).astype(jnp.float32)
    partial, output = lax.optimization_barrier((partial, output))

    routed = pl.pallas_call(
        route_kernel,
        out_shape=jax.ShapeDtypeStruct((2, slots // 2, feats), jnp.bfloat16),
        compiler_params=pltpu.CompilerParams(vmem_limit_bytes=16 * 1024 * 1024),
        cost_estimate=pl.CostEstimate(
            flops=2 * slots * tok * feats, bytes_accessed=2 << 20, transcendentals=0
        ),
        name="route",
    )(route, partial).reshape(owners_n, capacity, feats)
    routed = lax.all_to_all(
        routed, "seq", split_axis=0, concat_axis=0, tiled=True
    ).reshape(slots, feats)
    residual = ((output - routed.astype(jnp.float32)) * scale).astype(jnp.bfloat16)

    gradient = on_core(
        gradient_kernel,
        "gradient",
        jax.ShapeDtypeStruct((ZN, half // ZN, feats), jnp.bfloat16),
        4 * slots * half * feats,
        place,
        *ours,
        *theirs,
        residual,
        lax.ppermute(residual, "group", core_swap),
    )
    gradient = lax.all_to_all(
        gradient,
        "seq",
        split_axis=0,
        concat_axis=0,
        tiled=True,
        axis_index_groups=z_groups,
    )
    gradient = jnp.sum(gradient.astype(jnp.float32), axis=0).astype(jnp.bfloat16)

    passed = lax.ppermute(
        gradient,
        both,
        [(h * ZN + z, (3 - h) * ZN + z) for h in range(2) for z in range(ZN)],
    )
    whole = jnp.where(
        high == 0,
        jnp.concatenate([gradient, passed], axis=1),
        jnp.concatenate([passed, gradient], axis=1),
    )
    return jnp.where(group == 1, whole.astype(jnp.float32), 0.0)[None]


def solution(mesh):
    placed = (
        P("group", "seq", "tensor"),
        P("group", "seq", "tensor"),
        P("seq"),
        P("tensor", None),
        P(),
        P("seq", None),
        P("seq", "tensor"),
    )
    return jax.shard_map(
        shards, mesh=mesh, in_specs=placed, out_specs=P("group", "seq", "tensor"), check_vma=False
    )
```

```python
import functools

import jax
import jax.numpy as jnp
from jax import lax
from jax.experimental import pallas as pl
from jax.experimental.pallas import tpu as pltpu
from jax.sharding import PartitionSpec as P

HD = 128
ZN = 8
WINDOW = 9
PIECE = 272
LOW = -1e30


def partner_pairs(base):
    return [(base + i, base + (i + ZN) % (2 * ZN)) for i in range(2 * ZN)]


def attention_kernel(
    info, query, seg_query, mine, other, out, kept, seg_kept, stacked, scores, acc, top
):
    shard = info[0]
    core = info[1]
    tok = query.shape[0]
    heads = query.shape[1] // HD
    scale = (HD**-0.5) * 1.4426950408889634
    seg_q = seg_query[...]
    first_seg = seg_q[0:1, :][0, 0]

    upper = shard // ZN
    ring = lax.rem(shard, ZN)

    def keep_block(step, count):
        place = lax.rem(ring + 1 + step, ZN)
        place = jnp.where(step < ZN, place, step)
        block = jnp.where(place <= ring, upper * ZN + place, place)
        block = jnp.where(place == ZN, ring, block)
        block = jnp.where(place == ZN + 1, ring - 1, block)
        tail = mine[place, 256:272, :].astype(jnp.float32)
        last_seg = tail[1:2, HD - 1 : HD][0, 0]
        wanted = (block >= 0) & (block >= shard - WINDOW) & (block <= shard)
        wanted = wanted & (last_seg >= first_seg) & ((step < ZN) | (upper == 1))

        @pl.when(wanted)
        def _():
            first = mine[place, 0:256, :]
            second = other[place, 0:256, :]
            rows = pl.ds(pl.multiple_of(count * 256, 256), 256)
            kept[rows, 0:HD] = jnp.where(core == 0, first, second)
            kept[rows, HD : 2 * HD] = jnp.where(core == 0, second, first)
            seg_kept[count] = jnp.concatenate([tail[0:1, :], tail[1:2, :]], axis=1)

        return count + wanted.astype(jnp.int32)

    count = lax.fori_loop(ZN, ZN + 2, keep_block, jnp.int32(0))
    count = lax.fori_loop(0, ZN, keep_block, count)

    @pl.when(lax.rem(count, 2) == 1)
    def _():
        kept[pl.ds(pl.multiple_of(count * 256, 256), 256), :] = jnp.zeros(
            (256, 2 * HD), jnp.bfloat16
        )
        seg_kept[count] = jnp.full((1, 256), -1.0, jnp.float32)

    for head in range(heads):
        stacked[head * tok : (head + 1) * tok, :] = query[:, head * HD : (head + 1) * HD]
    top[...] = jnp.full_like(top, LOW)
    acc[...] = jnp.zeros_like(acc)
    causal = lax.broadcasted_iota(jnp.int32, (tok, 256), 1) <= lax.broadcasted_iota(
        jnp.int32, (tok, 256), 0
    )

    def score_pair(pair, carry):
        keys = kept[pl.ds(pl.multiple_of(pair * 512, 512), 512), 0:HD]
        found = lax.dot_general(
            stacked[...], keys, (((1,), (1,)), ((), ())), preferred_element_type=jnp.float32
        )
        for side in range(2):
            index = 2 * pair + side
            allowed = (seg_kept[index] == seg_q) & (causal | (index != count - 1))
            for head in range(heads):
                rows = slice(head * tok, (head + 1) * tok)
                part = jnp.where(allowed, found[rows, side * 256 : (side + 1) * 256], LOW)
                scores[index, rows, :] = part
                top[rows, :] = jnp.maximum(top[rows, :], jnp.maximum(part[:, :HD], part[:, HD:]))
        return carry

    pairs = (count + 1) // 2
    lax.fori_loop(0, pairs, score_pair, 0)
    top[...] = jnp.broadcast_to(jnp.max(top[...], axis=1, keepdims=True), top.shape)

    def mix_pair(pair, carry):
        values = kept[pl.ds(pl.multiple_of(pair * 512, 512), 512), HD : 2 * HD]
        values = jnp.concatenate([values, jnp.ones_like(values)], axis=1)
        best = jnp.concatenate([top[...], top[...]], axis=1)
        weights = jnp.concatenate(
            [
                jnp.exp2((scores[2 * pair + side] - best) * scale).astype(jnp.bfloat16)
                for side in range(2)
            ],
            axis=1,
        )
        acc[...] += jnp.dot(weights, values, preferred_element_type=jnp.float32)
        return carry

    lax.fori_loop(0, pairs, mix_pair, 0)
    for head in range(heads):
        mixed = acc[head * tok : (head + 1) * tok, :]
        out[:, head * HD : (head + 1) * HD] = (mixed[:, :HD] / mixed[:, HD:]).astype(jnp.bfloat16)


def attend(info, query, seg_query, mine, other):
    tok, width = query.shape
    heads = width // HD
    blocks = WINDOW + 1
    vmem = pl.BlockSpec(memory_space=pltpu.VMEM)
    return pl.pallas_call(
        attention_kernel,
        out_shape=jax.ShapeDtypeStruct((tok, width), jnp.bfloat16),
        in_specs=[pl.BlockSpec(memory_space=pltpu.SMEM)] + [pl.BlockSpec()] * 4,
        out_specs=vmem,
        scratch_shapes=[
            pltpu.VMEM((blocks * 256, 2 * HD), jnp.bfloat16),
            pltpu.VMEM((blocks, 1, 256), jnp.float32),
            pltpu.VMEM((heads * tok, HD), jnp.bfloat16),
            pltpu.VMEM((blocks, heads * tok, 256), jnp.float32),
            pltpu.VMEM((heads * tok, 2 * HD), jnp.float32),
            pltpu.VMEM((heads * tok, HD), jnp.float32),
        ],
        compiler_params=pltpu.CompilerParams(vmem_limit_bytes=24 * 1024 * 1024),
        cost_estimate=pl.CostEstimate(
            flops=8 * tok * width * 2560,
            bytes_accessed=4 << 20,
            transcendentals=tok * heads * 2560,
        ),
        name="attend",
    )(info, query, seg_query, mine, other)


def project_kernel(core, context, low, high, out):
    weight = jnp.concatenate([low[...], high[...]], axis=1)
    out[0] = jnp.dot(context[...], weight, preferred_element_type=jnp.float32).astype(jnp.bfloat16)


def project(core, context, projector, tensor_n):
    tok, width = context.shape
    feats = projector.shape[1] // (4 * tensor_n)
    return pl.pallas_call(
        project_kernel,
        out_shape=jax.ShapeDtypeStruct((tensor_n, tok, 2 * feats), jnp.bfloat16),
        grid_spec=pltpu.PrefetchScalarGridSpec(
            num_scalar_prefetch=1,
            grid=(tensor_n,),
            in_specs=[
                pl.BlockSpec((tok, width), lambda i, core: (0, 0)),
                pl.BlockSpec((width, feats), lambda i, core: (0, 4 * i + core[0])),
                pl.BlockSpec((width, feats), lambda i, core: (0, 4 * i + 2 + core[0])),
            ],
            out_specs=pl.BlockSpec((1, tok, 2 * feats), lambda i, core: (i, 0, 0)),
        ),
        compiler_params=pltpu.CompilerParams(vmem_limit_bytes=16 * 1024 * 1024),
        cost_estimate=pl.CostEstimate(
            flops=4 * tok * width * feats * tensor_n,
            bytes_accessed=4 * width * feats * tensor_n,
            transcendentals=0,
        ),
        name="project",
    )(core, context, projector, projector)


def route_kernel(route, partial, out):
    target = partial[0].astype(jnp.float32)
    for index in range(1, partial.shape[0]):
        target = target + partial[index].astype(jnp.float32)
    routed = jnp.dot(
        route[...], target.astype(jnp.bfloat16), preferred_element_type=jnp.float32
    ).astype(jnp.bfloat16)
    rows, lanes = out.shape[1], out.shape[2] // 2
    low, high = routed[:rows], routed[rows:]
    out[0] = jnp.concatenate([low[:, :lanes], high[:, :lanes]], axis=1)
    out[1] = jnp.concatenate([high[:, lanes:], low[:, lanes:]], axis=1)


def student_kernel(place, ours_low, ours_high, theirs_low, theirs_high, weight, kept, sent):
    core = place[1]
    middle = ours_low.shape[1]

    def product(low, high):
        return jnp.dot(
            low[...], weight[:middle, :], preferred_element_type=jnp.float32
        ) + jnp.dot(high[...], weight[middle:, :], preferred_element_type=jnp.float32)

    own = product(ours_low, ours_high)
    partner = product(theirs_low, theirs_high)
    lanes = own.shape[1] // 2
    first = jnp.concatenate([own[:, :lanes], partner[:, :lanes]], axis=1)
    second = jnp.concatenate([own[:, lanes:], partner[:, lanes:]], axis=1)
    kept[...] = jnp.where(core == 0, first, second)
    sent[...] = jnp.where(core == 0, second, first).astype(jnp.bfloat16)


def gradient_kernel(place, ours_low, ours_high, theirs_low, theirs_high, mine, other, out):
    core = place[1]
    lanes = mine.shape[1] // 2
    first = jnp.where(core == 0, mine[...], other[...])
    second = jnp.where(core == 0, other[...], mine[...])
    own = jnp.concatenate([first[:, :lanes], second[:, :lanes]], axis=1)
    partner = jnp.concatenate([first[:, lanes:], second[:, lanes:]], axis=1)
    over_rows = (((0,), (0,)), ((), ()))
    count, width = out.shape[0] // 2, out.shape[1]
    for side, (ours, theirs) in enumerate(((ours_low, theirs_low), (ours_high, theirs_high))):
        for index in range(count):
            columns = slice(index * width, (index + 1) * width)
            out[side * count + index] = (
                lax.dot_general(ours[:, columns], own, over_rows, preferred_element_type=jnp.float32)
                + lax.dot_general(
                    theirs[:, columns], partner, over_rows, preferred_element_type=jnp.float32
                )
            ).astype(jnp.bfloat16)


def on_core(kernel, name, out_shape, flops, place, *args):
    vmem = pl.BlockSpec(memory_space=pltpu.VMEM)
    return pl.pallas_call(
        kernel,
        out_shape=out_shape,
        in_specs=[pl.BlockSpec(memory_space=pltpu.SMEM)] + [vmem] * len(args),
        out_specs=jax.tree.map(lambda _: vmem, out_shape),
        compiler_params=pltpu.CompilerParams(vmem_limit_bytes=32 * 1024 * 1024),
        cost_estimate=pl.CostEstimate(flops=flops, bytes_accessed=6 << 20, transcendentals=0),
        name=name,
    )(place, *args)


def shards(
    teacher_query,
    teacher_keyval,
    segment_ids,
    projector,
    owner_table,
    student_context,
    student_out_weight,
):
    group = lax.axis_index("group")
    seq = lax.axis_index("seq")
    high = seq // ZN
    query = teacher_query[0]
    tok = query.shape[0]
    slots, model = student_context.shape
    owners_n = 2 * ZN
    capacity = slots // owners_n
    half = model // 2
    feats = student_out_weight.shape[1] // 2
    tensor_n = model // (2 * feats)
    z_groups = [[h * ZN + z for z in range(ZN)] for h in range(2)]

    core_swap = [(0, 1), (1, 0)]
    both = ("group", "seq")
    all_pairs = partner_pairs(0) + partner_pairs(owners_n)

    keyval = teacher_keyval[0]
    seg_rows = segment_ids.astype(jnp.bfloat16).reshape(2, HD)
    seg_rows = jnp.concatenate([seg_rows, jnp.zeros((14, HD), jnp.bfloat16)], axis=0)
    passed = lax.ppermute(keyval, "group", [(0, 1)])
    piece = jnp.where(group == 0, keyval[:, :HD], passed[:, HD:])
    piece = jnp.concatenate([piece, seg_rows], axis=0)
    piece, student_context = lax.optimization_barrier((piece, student_context))
    column_half = jnp.where(group == 1, high, 1 - high)
    crossing = lax.dynamic_slice_in_dim(student_out_weight, (1 - high) * feats, feats, axis=1)
    crossing = jnp.concatenate([crossing, jnp.zeros((16, feats), crossing.dtype)], axis=0)
    exchanged = lax.ppermute(jnp.concatenate([crossing, piece], axis=1), both, all_pairs)
    lower = exchanged[:, feats:]
    crossing = exchanged[:256, :feats]
    ring = seq % ZN
    later = (jnp.arange(ZN, dtype=jnp.int32) >= ring) | (high == 0)
    pieces = jnp.where(later[:, None, None], piece[None], lower[None])
    def column_parts(rows, place):
        return [
            lax.dynamic_slice_in_dim(rows, place * half + side * (half // 2), half // 2, axis=1)
            for side in range(2)
        ]

    sent = column_parts(student_context, 1 - column_half)
    pieces, query, sent, student_context, student_out_weight, owner_table = (
        lax.optimization_barrier(
            (pieces, query, sent, student_context, student_out_weight, owner_table)
        )
    )
    mine = lax.all_to_all(
        pieces, "seq", split_axis=0, concat_axis=0, tiled=True, axis_index_groups=z_groups
    )

    theirs = [lax.ppermute(part, both, all_pairs) for part in sent]

    width = query.shape[1] // 2
    other_query = lax.ppermute(query[:, width:], "group", [(0, 1)])
    weight = lax.dynamic_slice_in_dim(student_out_weight, high * feats, feats, axis=1)
    weight = jnp.where(group == 1, weight, crossing)
    weight = jnp.broadcast_to(weight[None], (ZN,) + weight.shape)
    other_query, lower, weight = lax.optimization_barrier((other_query, lower, weight))
    below = lax.ppermute(
        lower,
        both,
        [
            (g * 2 * ZN + ZN + z, g * 2 * ZN + ZN + z + 1)
            for g in range(2)
            for z in range(ZN - 1)
        ],
    )
    query = jnp.where(group == 0, query[:, :width], other_query)
    seg_query = segment_ids.astype(jnp.float32)[:, None]
    info = jnp.stack([seq, group]).astype(jnp.int32)

    owners_all = owner_table[:, 0]
    owners = lax.dynamic_slice_in_dim(owners_all, seq * tok, tok)
    index = jnp.arange(tok, dtype=jnp.int32)
    ranks = jnp.sum(
        ((owners[:, None] == owners[None, :]) & (index[None, :] < index[:, None])).astype(
            jnp.int32
        ),
        axis=1,
    )
    slot = owners * capacity + ranks
    route = (jnp.arange(slots, dtype=jnp.int32)[:, None] == slot[None, :]).astype(jnp.bfloat16)
    pair_owners = jnp.stack([seq, (seq + ZN) % owners_n])
    counts = jnp.sum(
        (owners_all.reshape(owners_n, tok, 1) == pair_owners[None, None, :]).astype(jnp.int32),
        axis=1,
    )
    live = jnp.arange(capacity, dtype=jnp.int32)[None, :, None] < counts[:, None, :]
    scale = live.reshape(slots, 2, 1).astype(jnp.float32) / tok
    scale = jnp.broadcast_to(scale, (slots, 2, feats // 2)).reshape(slots, feats)
    mine, weight, below, query, seg_query, info, route, scale = lax.optimization_barrier(
        (mine, weight, below, query, seg_query, info, route, scale)
    )
    weight = lax.all_to_all(
        weight, "seq", split_axis=0, concat_axis=0, tiled=True, axis_index_groups=z_groups
    ).reshape(half, feats)
    mine = jnp.concatenate([mine, lower[None], below[None]], axis=0)
    mine, theirs[0] = lax.optimization_barrier((mine, theirs[0]))
    other = lax.ppermute(mine, "group", core_swap)
    context = attend(info, query, seg_query, mine, other)
    place = info
    ours = column_parts(student_context, column_half)

    other_context = lax.ppermute(context, "group", core_swap)
    context = jnp.where(
        group == 0,
        jnp.concatenate([context, other_context], axis=1),
        jnp.concatenate([other_context, context], axis=1),
    )
    partial = project(group[None].astype(jnp.int32), context, projector, tensor_n)
    partial, theirs[1] = lax.optimization_barrier((partial, theirs[1]))
    partial = lax.all_to_all(partial, "tensor", split_axis=0, concat_axis=0, tiled=True)
    output, given = on_core(
        student_kernel,
        "student",
        [
            jax.ShapeDtypeStruct((slots, feats), jnp.float32),
            jax.ShapeDtypeStruct((slots, feats), jnp.bfloat16),
        ],
        4 * slots * half * feats,
        place,
        *ours,
        *theirs,
        weight,
    )
    output = output + lax.ppermute(given, "group", core_swap).astype(jnp.float32)
    partial, output = lax.optimization_barrier((partial, output))

    routed = pl.pallas_call(
        route_kernel,
        out_shape=jax.ShapeDtypeStruct((2, slots // 2, feats), jnp.bfloat16),
        compiler_params=pltpu.CompilerParams(vmem_limit_bytes=16 * 1024 * 1024),
        cost_estimate=pl.CostEstimate(
            flops=2 * slots * tok * feats, bytes_accessed=2 << 20, transcendentals=0
        ),
        name="route",
    )(route, partial).reshape(owners_n, capacity, feats)
    routed = lax.all_to_all(
        routed, "seq", split_axis=0, concat_axis=0, tiled=True
    ).reshape(slots, feats)
    residual = ((output - routed.astype(jnp.float32)) * scale).astype(jnp.bfloat16)

    gradient = on_core(
        gradient_kernel,
        "gradient",
        jax.ShapeDtypeStruct((ZN, half // ZN, feats), jnp.bfloat16),
        4 * slots * half * feats,
        place,
        *ours,
        *theirs,
        residual,
        lax.ppermute(residual, "group", core_swap),
    )
    gradient = lax.all_to_all(
        gradient,
        "seq",
        split_axis=0,
        concat_axis=0,
        tiled=True,
        axis_index_groups=z_groups,
    )
    gradient = jnp.sum(gradient.astype(jnp.float32), axis=0).astype(jnp.bfloat16)

    passed = lax.ppermute(
        gradient,
        both,
        [(h * ZN + z, (3 - h) * ZN + z) for h in range(2) for z in range(ZN)],
    )
    whole = jnp.where(
        high == 0,
        jnp.concatenate([gradient, passed], axis=1),
        jnp.concatenate([passed, gradient], axis=1),
    )
    return jnp.where(group == 1, whole.astype(jnp.float32), 0.0)[None]


def solution(mesh):
    placed = (
        P("group", "seq", "tensor"),
        P("group", "seq", "tensor"),
        P("seq"),
        P("tensor", None),
        P(),
        P("seq", None),
        P("seq", "tensor"),
    )
    return jax.shard_map(
        shards, mesh=mesh, in_specs=placed, out_specs=P("group", "seq", "tensor"), check_vma=False
    )
```
